512 devices in a mesh: dp: 32 (over y, z_hi, core), feat: 16 (over z_lo, x).
Axes of the slice: x: 4, y: 4, z: 16 (z_hi: 4, z_lo: 4; z = z_hi * 4 + z_lo), core: 2. Of those that a mesh axis runs over, the one named last changes fastest.
Arguments:
- h_a: bfloat16 [4096, 4096], P('dp', 'feat'), may hold values from -6 to 6
- h_b: bfloat16 [4096, 4096], P('dp', 'feat'), may hold values from -6 to 6
- z_a: bfloat16 [4096, 4096], P('dp', 'feat'), may hold values from -700 to 700
- z_b: bfloat16 [4096, 4096], P('dp', 'feat'), may hold values from -700 to 700
Outputs:
- weight_grad: float32 [16, 32, 8, 4096], P(None, 'dp', None, 'feat')
The draws below stay inside these ranges and needn't reach their ends.
All inputs are finite; a program needn't handle non-finite values.
Results may differ from the reference program's by a relative error of at most 0.034.
Values may be sent and summed in bfloat16 or wider, within the bound.
No kernel may reach another device: no remote copies, remote signals or barrier semaphores. Data moves between devices by JAX's collectives and lax.ppermute only.
A program may use at most 64 MiB of HBM per device.

```python
import jax
import jax.numpy as jnp
from jax import lax

D = 4096
PAIRS = 4096
N_DP = 32
N_FEAT = 16


def shared_part(key):
    return jnp.clip(jax.random.normal(jax.random.fold_in(key, 7), (PAIRS, D), jnp.float32), -5.0, 5.0)


def column_law(key, top):
    first, second = jax.random.split(key)
    scale = jnp.exp(jax.random.uniform(first, (D,), jnp.float32) * jnp.log(top))
    shift = 0.5 * scale * jnp.clip(jax.random.normal(second, (D,), jnp.float32), -5.0, 5.0)
    return (scale, shift)


def draw_z_a(key, part):
    shared = shared_part(key)
    key = jax.random.fold_in(key, 1)
    first = jax.random.fold_in(key, 0)
    scale, shift = column_law(first, 10.0)
    values = shared
    return (values * scale + shift).astype(jnp.bfloat16)


def draw_z_b(key, part):
    shared = shared_part(key)
    key = jax.random.fold_in(key, 2)
    first = jax.random.fold_in(key, 0)
    third = jax.random.fold_in(key, 2)
    noise = jnp.clip(jax.random.normal(third, (PAIRS, D), jnp.float32), -5.0, 5.0)
    scale, shift = column_law(first, 10.0)
    values = 0.98 * shared + 0.2 * noise
    return (values * scale + shift).astype(jnp.bfloat16)


def level_of(own_key, dims, cuts, least, high):
    loudness = 1.0
    for position, shards_of in cuts:
        steps = jax.random.uniform(jax.random.fold_in(jax.random.fold_in(own_key, 6), position), (shards_of,), jnp.float32, least / len(cuts), high / len(cuts))
        loudness = loudness * jnp.repeat(jnp.exp(steps), dims[position] // shards_of).reshape((-1,) + (1,) * (len(dims) - 1 - position))
    return loudness


def scatter_about(key, extent, scale, reach, cuts=(), kind=jnp.bfloat16):
    drawn = scale * jax.random.normal(key, extent, jnp.float32)
    if cuts:
        drawn = drawn * level_of(key, extent, cuts, -0.22, 0.18)
    return jnp.clip(drawn, -reach, reach).astype(kind)


def setup_inputs(seed: int = 0) -> dict:
    seeds = jax.random.split(jax.random.key(seed), 5)
    h_a = scatter_about(seeds[0], (PAIRS, D), 1.0, 6.0, ((0, 32), (1, 16)))
    h_b = scatter_about(seeds[1], (PAIRS, D), 1.0, 6.0, ((0, 32), (1, 16)))
    z_a = draw_z_a(jax.random.fold_in(seeds[4], 71), 0)
    z_b = draw_z_b(jax.random.fold_in(seeds[4], 71), 0)
    return {"h_a": h_a, "h_b": h_b, "z_a": z_a, "z_b": z_b}


epsilon = 1e-05
off_weight = 0.0051

def normalize(values):
    floats = values.astype(jnp.float32)
    col_mean = lax.optimization_barrier(jnp.sum(floats, axis=0)) / PAIRS
    variance = lax.optimization_barrier(jnp.sum(floats * floats, axis=0)) / PAIRS - col_mean * col_mean
    inverse = lax.rsqrt(variance + epsilon)
    return (((floats - col_mean) * inverse).astype(jnp.bfloat16), inverse)

def norm_back(upstream, normed, inverse):
    floats = normed.astype(jnp.float32)
    first = lax.optimization_barrier(jnp.sum(upstream, axis=0)) / PAIRS
    second = lax.optimization_barrier(jnp.sum(upstream * floats, axis=0)) / PAIRS
    return (inverse * (upstream - first - floats * second)).astype(jnp.bfloat16)

def reference(h_a, h_b, z_a, z_b):
    zn_a, inv_a = normalize(z_a)
    zn_b, inv_b = normalize(z_b)
    floats_a = zn_a.astype(jnp.float32)
    floats_b = zn_b.astype(jnp.float32)
    correlation = jnp.dot(floats_a.T, floats_b) / PAIRS
    index_all = jnp.arange(D, dtype=jnp.int32)
    on_diagonal = index_all[:, None] == index_all[None, :]
    diagonal = lax.optimization_barrier(jnp.sum(jnp.where(on_diagonal, correlation, 0.0), axis=1))
    grad_corr = jnp.where(on_diagonal, (-2.0 * (1.0 - diagonal))[:, None], 2.0 * off_weight * correlation).astype(jnp.bfloat16)
    grad_floats = grad_corr.astype(jnp.float32)
    block_width = D // N_FEAT
    sub_width = D // (N_FEAT * N_DP)
    shaped_b = floats_b.reshape(PAIRS, N_FEAT, N_DP, sub_width)
    shaped_g = grad_floats.reshape(D, N_FEAT, N_DP, sub_width)

    def add_a(group, total):
        picked_b = lax.dynamic_slice_in_dim(shaped_b, group, 1, 2).reshape(PAIRS, N_FEAT * sub_width)
        picked_g = lax.dynamic_slice_in_dim(shaped_g, group, 1, 2).reshape(D, N_FEAT * sub_width)
        term = jnp.dot(picked_b, picked_g.T) / PAIRS
        rounded = lax.optimization_barrier(term.astype(jnp.bfloat16))
        return total + rounded.astype(jnp.float32)

    def add_b(group, total):
        start = group * block_width
        part_a = lax.dynamic_slice_in_dim(floats_a, start, block_width, 1)
        part_g = lax.dynamic_slice_in_dim(grad_floats, start, block_width, 0)
        term = jnp.dot(part_a, part_g) / PAIRS
        rounded = lax.optimization_barrier(term.astype(jnp.bfloat16))
        return total + rounded.astype(jnp.float32)
    dzn_a = lax.fori_loop(0, N_DP, add_a, jnp.zeros((PAIRS, D), jnp.float32))
    dzn_b = lax.fori_loop(0, N_FEAT, add_b, jnp.zeros((PAIRS, D), jnp.float32))
    dz_a = norm_back(dzn_a, zn_a, inv_a).astype(jnp.float32)
    dz_b = norm_back(dzn_b, zn_b, inv_b).astype(jnp.float32)
    weight_grad = (jnp.dot(h_a.astype(jnp.float32).T, dz_a) + jnp.dot(h_b.astype(jnp.float32).T, dz_b)) * PAIRS
    return weight_grad.reshape(N_FEAT, N_DP, sub_width, D)
```

```python
import jax
import jax.numpy as jnp
from jax import lax
from jax.sharding import Mesh, PartitionSpec as P

epsilon = 1e-05
off_weight = 0.0051

SIZES = (("y", 4), ("zh", 4), ("c", 2), ("zl", 4), ("x", 4))
DP = ("y", "zh", "c")
FEAT = ("zl", "x")
bf16 = jnp.bfloat16
f32 = jnp.float32


def gather(block, axis):
    count = lax.axis_size(axis)
    copies = jnp.broadcast_to(block[None], (count, *block.shape))
    return lax.all_to_all(copies, axis, 0, 0, tiled=True)


def stats(total, squares, pair_count):
    mean = total / pair_count
    variance = squares / pair_count - mean * mean
    return mean, lax.rsqrt(variance + epsilon)


def dot(left, right, dims):
    return lax.dot_general(left, right, (dims, ((), ())), preferred_element_type=f32)


def body(h_a, h_b, z_a, z_b):
    local_rows, width = z_a.shape
    n_dp = lax.axis_size(DP)
    n_feat = lax.axis_size(FEAT)
    n_y, n_zh, n_c = (lax.axis_size(a) for a in DP)
    n_zl, n_x = (lax.axis_size(a) for a in FEAT)
    pairs = local_rows * n_dp
    sub = width // n_dp
    owned = n_feat * sub

    with jax.named_scope("columns"):
        cut = jnp.stack([v.T.reshape(n_dp, sub, local_rows) for v in (z_b, h_a, h_b)], axis=1)
        cut = lax.all_to_all(cut, DP, 0, 0, tiled=True)
        cut = cut.reshape(n_y, n_zh, n_c, 3, sub, local_rows)
        cut = cut.transpose(3, 4, 2, 0, 1, 5).reshape(3, sub, pairs)

    with jax.named_scope("rows"):
        rows = jnp.concatenate([z_a, z_b], axis=1)
        rows = gather(rows, "zh")
        rows = gather(rows, "y")
        rows = gather(rows, "c").reshape(pairs, 2 * width)

    with jax.named_scope("cols_b"):
        cols_b = gather(gather(cut[0], "zl"), "x").reshape(owned, pairs)
    with jax.named_scope("cols_h"):
        cols_h = gather(gather(cut[1:], "zl"), "x").reshape(2 * owned, pairs)

    with jax.named_scope("normalize"):
        floats = rows.astype(f32)
        mean, inverse = stats(jnp.sum(floats, 0), jnp.sum(floats * floats, 0), pairs)
        normed = ((floats - mean) * inverse).astype(bf16)
        floats_b = cols_b.astype(f32)
        mean_b, inverse_b = stats(jnp.sum(floats_b, 1), jnp.sum(floats_b * floats_b, 1), pairs)
        normed_b = ((floats_b - mean_b[:, None]) * inverse_b[:, None]).astype(bf16)

    with jax.named_scope("grad"):
        corr = dot(normed_b, normed[:, :width], ((1,), (0,))) / pairs
        f_index = lax.axis_index(FEAT)
        p_index = lax.axis_index(DP)
        lane = lax.broadcasted_iota(jnp.int32, (owned, width), 1)
        row = lax.broadcasted_iota(jnp.int32, (owned, width), 0)
        row_f = (row // sub % n_zl) * n_x + row // (sub * n_zl)
        diagonal = (row_f == f_index) & (p_index * sub + row % sub == lane)
        grad = jnp.where(diagonal, -2.0 * (1.0 - corr), 2.0 * off_weight * corr).astype(bf16)

    with jax.named_scope("grad_rows"):
        grads = gather(gather(gather(grad, "zh"), "y"), "c")
        grads = grads.reshape(n_c, n_y, n_zh, n_x, n_zl, sub, width)
        grads = grads.transpose(3, 4, 1, 2, 0, 5, 6).reshape(n_x, n_zl, width, width)

    with jax.named_scope("products"):
        prod = dot(cols_h, normed, ((1,), (0,))).reshape(n_x, n_zl, 2, sub, 2, width)
        h_sum = jnp.sum(cols_h.astype(f32), 1).reshape(n_x, n_zl, 2, sub)
        h_sum = h_sum.transpose(2, 0, 1, 3).reshape(2, owned)
        z_sum = jnp.sum(normed.astype(f32), 0).reshape(2, width)
        prod = prod.transpose(2, 4, 0, 1, 3, 5).reshape(2, 2, owned, width)
        p_ab = (prod[0, 1] - h_sum[0][:, None] * z_sum[1] / pairs).astype(bf16)
        p_ba = (prod[1, 0] - h_sum[1][:, None] * z_sum[0] / pairs).astype(bf16)
        p_ab_all = gather(gather(p_ab.T, "zl"), "x").reshape(n_feat * width, owned)

    with jax.named_scope("moments"):
        g = grads.astype(f32)
        four = lambda d: lax.broadcasted_iota(jnp.int32, g.shape, d)
        on = (four(1) * n_x + four(0) == f_index) & (four(2) == four(3))
        weighed = g * jnp.where(on, 1.0 + 0.5 * g, g * (0.5 / off_weight)) / pairs
        second_a = jnp.sum(weighed, (0, 1, 2))
        part_b = jnp.sum(weighed, 3)

    with jax.named_scope("weight_b"):
        flat = grads.reshape(n_feat * width, width)
        w_b = dot(flat, p_ba, ((1,), (1,))).astype(bf16).reshape(n_x, n_zl, width, owned)

        def with_moments(w, m):
            high = m.astype(bf16)
            low = (m - high.astype(f32)).astype(bf16)
            lead = m.shape[:-1]
            extra = jnp.concatenate(
                [high.reshape(*lead, -1, owned), low.reshape(*lead, -1, owned)], axis=-2
            )
            pad = jnp.zeros((*lead, 16 - extra.shape[-2], owned), bf16)
            return jnp.concatenate([w, extra, pad], axis=-2)

        def parted(total):
            n_extra = width // owned
            m = total[..., width : width + n_extra, :] + total[..., width + n_extra : width + 2 * n_extra, :]
            return total[..., :width, :], m.reshape(*m.shape[:-2], width)

        got = lax.all_to_all(with_moments(w_b, part_b), "x", 0, 0, tiled=True)
        w, m = parted(jnp.sum(got.astype(f32), 0))
        got = lax.all_to_all(with_moments(w.astype(bf16), m), "zl", 0, 0, tiled=True)
        w_b, second_b = parted(jnp.sum(got.astype(f32), 0))

    with jax.named_scope("weight_a"):
        w_a = dot(p_ab_all, flat, ((0,), (0,)))

    with jax.named_scope("finish"):
        inv_a, inv_b = inverse[:width], inverse[width:]
        result = inv_a * (w_a - pairs * prod[0, 0] * second_a)
        result = result + inv_b * (w_b.T - pairs * prod[1, 1] * second_b)
        result = result.reshape(n_x, n_zl, sub, width).transpose(1, 0, 2, 3)
        return result.reshape(n_feat, 1, sub, width)


def solution(mesh):
    names = tuple(n for n, _ in SIZES)
    fine = Mesh(mesh.devices.reshape(tuple(s for _, s in SIZES)), names)
    spec = P(DP, FEAT)
    return jax.shard_map(
        body,
        mesh=fine,
        in_specs=(spec, spec, spec, spec),
        out_specs=P(None, DP, None, FEAT),
        check_vma=False,
    )
```

```python
import jax
import jax.numpy as jnp
from jax import lax
from jax.experimental import pallas as pl
from jax.experimental.pallas import tpu as pltpu
from jax.sharding import Mesh, PartitionSpec as P

epsilon = 1e-05
off_weight = 0.0051

SIZES = (("y", 4), ("zh", 4), ("c", 2), ("zl", 4), ("x", 4))
DP = ("y", "zh", "c")
FEAT = ("zl", "x")
bf16 = jnp.bfloat16
f32 = jnp.float32


def gather(block, axis):
    count = lax.axis_size(axis)
    copies = jnp.broadcast_to(block[None], (count, *block.shape))
    return lax.all_to_all(copies, axis, 0, 0, tiled=True)


def stats(total, squares, pair_count):
    mean = total / pair_count
    variance = squares / pair_count - mean * mean
    return mean, lax.rsqrt(variance + epsilon)


def dot(left, right, dims):
    return lax.dot_general(left, right, (dims, ((), ())), preferred_element_type=f32)


def collect(block, axis):
    return lax.all_gather(block, axis, axis=0, tiled=False)


STEP = 256


def at(i):
    return pl.ds(pl.multiple_of(i * STEP, STEP), STEP)


def fold(v):
    return jnp.sum(v.reshape(v.shape[0] // 8, 8, v.shape[1]), 0)


def lanes(v):
    return v[:, :128] + v[:, 128:]


def chunk(halves, side, i):
    own, other = halves
    count = own.shape[0] * own.shape[2] // STEP
    each = STEP // own.shape[2]
    ref = own if i < count else other
    first = (i % count) * each
    return jnp.concatenate([ref[first + j, side] for j in range(each)], axis=0)


def column_stats(halves, side, pairs):
    width = halves[0].shape[3]
    total = squares = jnp.zeros((8, width), f32)
    for i in range(pairs // STEP):
        v = chunk(halves, side, i).astype(f32)
        total, squares = total + fold(v), squares + fold(v * v)
    return stats(jnp.sum(total, 0, keepdims=True), jnp.sum(squares, 0, keepdims=True), pairs)


def row_stats(cols_ref):
    owned, pairs = cols_ref.shape

    def add(i, carry):
        v = cols_ref[:, at(i)].astype(f32)
        return carry[0] + lanes(v), carry[1] + lanes(v * v)

    empty = jnp.zeros((owned, 128), f32)
    total, squares = lax.fori_loop(0, pairs // STEP, add, (empty, empty))
    return stats(jnp.sum(total, 1, keepdims=True), jnp.sum(squares, 1, keepdims=True), pairs)


def normalize(v, mean, inverse):
    return ((v.astype(f32) - mean) * inverse).astype(bf16)


def matmul(left, right):
    return jnp.dot(left, right, preferred_element_type=f32)


def grad_kernel(own_ref, other_ref, cols_ref, target_ref, grad_ref, stats_ref):
    owned, pairs = cols_ref.shape
    halves = (own_ref, other_ref)
    width = grad_ref.shape[1]
    mean, inverse = column_stats(halves, 0, pairs)
    mean_b, inverse_b = row_stats(cols_ref)
    stats_ref[0:8, :] = jnp.broadcast_to(mean, (8, width))
    stats_ref[8:16, :] = jnp.broadcast_to(inverse, (8, width))
    corr = jnp.zeros((owned, width), f32)
    for i in range(pairs // STEP):
        v = normalize(chunk(halves, 0, i), mean, inverse)
        b = normalize(cols_ref[:, pl.ds(i * STEP, STEP)], mean_b, inverse_b)
        corr = corr + matmul(b, v)
    corr = corr / pairs
    diagonal = lax.broadcasted_iota(jnp.int32, (owned, width), 1) == target_ref[...]
    grad_ref[...] = jnp.where(diagonal, -2.0 * (1.0 - corr), 2.0 * off_weight * corr).astype(bf16)


def product_kernel(cols_ref, own_ref, other_ref, stats_ref, prod_ref, centered_ref, inverse_ref):
    owned, pairs = cols_ref.shape
    halves = (own_ref, other_ref)
    width = own_ref.shape[3]
    mean_a, inverse_a = stats_ref[0:1, :], stats_ref[8:9, :]
    mean_b, inverse_b = column_stats(halves, 1, pairs)
    inverse_ref[...] = jnp.broadcast_to(inverse_b, (8, width))
    prod_a = prod_b = jnp.zeros((owned, width), f32)
    sum_a = sum_b = jnp.zeros((8, width), f32)
    sum_h = jnp.zeros((owned, 128), f32)
    for i in range(pairs // STEP):
        h = cols_ref[:, pl.ds(i * STEP, STEP)]
        a = normalize(chunk(halves, 0, i), mean_a, inverse_a)
        b = normalize(chunk(halves, 1, i), mean_b, inverse_b)
        prod_a, prod_b = prod_a + matmul(h, a), prod_b + matmul(h, b)
        sum_a, sum_b = sum_a + fold(a.astype(f32)), sum_b + fold(b.astype(f32))
        sum_h = sum_h + lanes(h.astype(f32))
    sum_h = jnp.sum(sum_h, 1, keepdims=True)
    for side, prod, sums in ((0, prod_a, sum_a), (1, prod_b, sum_b)):
        part = pl.ds(side * width, width)
        sums = jnp.sum(sums, 0, keepdims=True) / pairs
        prod_ref[:, part] = prod
        centered_ref[:, part] = (prod - sum_h * sums).astype(bf16)


def call(kernel, name, flops, shapes, *operands):
    size = lambda v: v.size * v.dtype.itemsize
    moved = sum(size(v) for v in operands) + sum(size(v) for v in shapes)
    return pl.pallas_call(
        kernel,
        out_shape=shapes,
        in_specs=[pl.BlockSpec(memory_space=pltpu.VMEM)] * len(operands),
        out_specs=[pl.BlockSpec(memory_space=pltpu.VMEM)] * len(shapes),
        compiler_params=pltpu.CompilerParams(vmem_limit_bytes=32 * 2**20),
        cost_estimate=pl.CostEstimate(flops=flops, bytes_accessed=moved, transcendentals=0),
        name=name,
    )(*operands)


def body(h_a, h_b, z_a, z_b):
    local_rows, width = z_a.shape
    n_dp = lax.axis_size(DP)
    n_feat = lax.axis_size(FEAT)
    n_y, n_zh, n_c = (lax.axis_size(a) for a in DP)
    n_zl, n_x = (lax.axis_size(a) for a in FEAT)
    pairs = local_rows * n_dp
    sub = width // n_dp
    owned = n_feat * sub
    shape = jax.ShapeDtypeStruct
    together = lax.optimization_barrier

    core = lax.axis_index("c")

    def swap(v):
        return lax.ppermute(v, "c", [(0, 1), (1, 0)])

    with jax.named_scope("columns"):
        cut = jnp.stack([v.T.reshape(n_dp, sub, local_rows) for v in (z_b, h_a, h_b)], axis=1)
        cut = lax.all_to_all(cut, DP, 0, 0, tiled=True)
    with jax.named_scope("rows"):
        rows = collect(jnp.stack([z_a, z_b]), "zh")
    cut, rows = together((cut, rows))
    with jax.named_scope("columns"):
        cut = cut.reshape(n_y, n_zh, n_c, 3, sub, local_rows)
        cut = jnp.where(core == 0, cut, jnp.flip(cut, 2))
        cut = cut.transpose(3, 4, 2, 0, 1, 5).reshape(3, sub, pairs)

    with jax.named_scope("rows"):
        rows = collect(rows, "y")
    with jax.named_scope("columns"):
        cut = collect(cut, "zl")
        cols_b = gather(cut[:, 0], "x").reshape(owned, pairs)
    rows, cols_b, cut = together((rows, cols_b, cut))
    with jax.named_scope("columns"):
        cols_h = collect(cut[:, 1:], "x").reshape(2 * owned, pairs)
    with jax.named_scope("rows"):
        own = rows.reshape(n_y * n_zh, 2, local_rows, width)
        other = swap(own)

    with jax.named_scope("grad"):
        f_index = lax.axis_index(FEAT)
        p_index = lax.axis_index(DP)
        row = lax.broadcasted_iota(jnp.int32, (owned, 1), 0)
        row_f = (row // sub % n_zl) * n_x + row // (sub * n_zl)
        target = jnp.where(row_f == f_index, p_index * sub + row % sub, -1)
        grad, stats_a = call(
            grad_kernel, "grad_block", 2 * pairs * owned * width,
            (shape((owned, width), bf16), shape((16, width), f32)),
            own, other, cols_b, target,
        )

    with jax.named_scope("grad_rows"):
        grads = gather(grad, "zh")
    grads, cols_h = together((grads, cols_h))

    with jax.named_scope("grad_rows"):
        grads = gather(grads, "y")
    with jax.named_scope("products"):
        prod, centered, inverse_b = call(
            product_kernel, "products", 8 * pairs * owned * width,
            (shape((2 * owned, 2 * width), f32), shape((2 * owned, 2 * width), bf16), shape((8, width), f32)),
            cols_h, own, other, stats_a,
        )
        halves = lambda v: v.reshape(n_x * n_zl, 2, sub, 2 * width)
        prod, centered = halves(prod), halves(centered)
        p_aa = prod[:, 0, :, :width].reshape(owned, width)
        p_bb = prod[:, 1, :, width:].reshape(owned, width)
        p_ab = centered[:, 0, :, width:].reshape(owned, width)
        p_ba = centered[:, 1, :, :width].reshape(owned, width)
        p_ab_all = collect(p_ab, "zl")
    grads, p_ab_all, p_ba = together((grads, p_ab_all, p_ba))

    with jax.named_scope("grad_rows"):
        grads = gather(grads, "c")
        grads = grads.reshape(n_c, n_y, n_zh, n_x, n_zl, sub, width)
        grads = grads.transpose(3, 4, 1, 2, 0, 5, 6).reshape(n_x, n_zl, width, width)
    with jax.named_scope("products"):
        p_ab_all = collect(p_ab_all, "x")

    with jax.named_scope("moments"):
        g = grads.astype(f32)
        four = lambda d: lax.broadcasted_iota(jnp.int32, g.shape, d)
        on = (four(1) * n_x + four(0) == f_index) & (four(2) == four(3))
        weighed = g * jnp.where(on, 1.0 + 0.5 * g, g * (0.5 / off_weight)) / pairs
        second_a = jnp.sum(weighed, (0, 1, 2))
        part_b = jnp.sum(weighed, 3)

    with jax.named_scope("weight_b"):
        flat = grads.reshape(n_feat * width, width)
        w_b = dot(flat, p_ba, ((1,), (1,))).astype(bf16).reshape(n_x, n_zl, width, owned)

        def with_moments(w, m):
            high = m.astype(bf16)
            low = (m - high.astype(f32)).astype(bf16)
            lead = m.shape[:-1]
            extra = jnp.concatenate(
                [high.reshape(*lead, -1, owned), low.reshape(*lead, -1, owned)], axis=-2
            )
            pad = jnp.zeros((*lead, 16 - extra.shape[-2], owned), bf16)
            return jnp.concatenate([w, extra, pad], axis=-2)

        def parted(total):
            n_extra = width // owned
            m = total[..., width : width + n_extra, :] + total[..., width + n_extra : width + 2 * n_extra, :]
            return total[..., :width, :], m.reshape(*m.shape[:-2], width)

        got = lax.all_to_all(with_moments(w_b, part_b), "x", 0, 0, tiled=True)
        w, m = parted(jnp.sum(got.astype(f32), 0))
        got = lax.all_to_all(with_moments(w.astype(bf16), m), "zl", 0, 0, tiled=True)
        w_b, second_b = parted(jnp.sum(got.astype(f32), 0))

    with jax.named_scope("weight_a"):
        w_a = dot(p_ab_all, grads, ((0, 1, 3), (0, 1, 2)))

    with jax.named_scope("finish"):
        inv_a, inv_b = stats_a[8], inverse_b[0]
        result = inv_a * (w_a - pairs * p_aa * second_a)
        result = result + inv_b * (w_b.T - pairs * p_bb * second_b)
        result = result.reshape(n_x, n_zl, sub, width).transpose(1, 0, 2, 3)
        return result.reshape(n_feat, 1, sub, width)


def solution(mesh):
    names = tuple(n for n, _ in SIZES)
    fine = Mesh(mesh.devices.reshape(tuple(s for _, s in SIZES)), names)
    spec = P(DP, FEAT)
    return jax.shard_map(
        body,
        mesh=fine,
        in_specs=(spec, spec, spec, spec),
        out_specs=P(None, DP, None, FEAT),
        check_vma=False,
    )
```

```python
import jax
import jax.numpy as jnp
from jax import lax
from jax.experimental import pallas as pl
from jax.experimental.pallas import tpu as pltpu
from jax.sharding import Mesh, PartitionSpec as P

epsilon = 1e-05
off_weight = 0.0051

SIZES = (("y", 4), ("zh", 4), ("c", 2), ("zl", 4), ("x", 4))
DP = ("y", "zh", "c")
FEAT = ("zl", "x")
bf16 = jnp.bfloat16
f32 = jnp.float32


def gather(block, axis):
    count = lax.axis_size(axis)
    copies = jnp.broadcast_to(block[None], (count, *block.shape))
    return lax.all_to_all(copies, axis, 0, 0, tiled=True)


def stats(total, squares, pair_count):
    mean = total / pair_count
    variance = squares / pair_count - mean * mean
    return mean, lax.rsqrt(variance + epsilon)


def dot(left, right, dims):
    return lax.dot_general(left, right, (dims, ((), ())), preferred_element_type=f32)


def collect(block, axis):
    return lax.all_gather(block, axis, axis=0, tiled=False)


STEP = 256


def fold(v):
    return jnp.sum(v.reshape(v.shape[0] // 8, 8, v.shape[1]), 0)


def lanes(v):
    return v[:, :128] + v[:, 128:]


def chunk(halves, side, i):
    own, other = halves
    count = own.shape[0] * own.shape[2] // STEP
    each = STEP // own.shape[2]
    ref = own if i < count else other
    first = (i % count) * each
    return jnp.concatenate([ref[first + j, side] for j in range(each)], axis=0)


def columns(cols_ref, views, i):
    at = pl.ds(i * STEP, STEP)
    return jnp.concatenate([cols_ref[x, v, :, at] for x in range(cols_ref.shape[0]) for v in views], axis=0)


def column_stats(halves, side, pairs):
    width = halves[0].shape[3]
    total = squares = jnp.zeros((8, width), f32)
    for i in range(pairs // STEP):
        v = chunk(halves, side, i).astype(f32)
        total, squares = total + fold(v), squares + fold(v * v)
    return stats(jnp.sum(total, 0, keepdims=True), jnp.sum(squares, 0, keepdims=True), pairs)


def row_stats(cols_ref, view, pairs):
    total = squares = 0.0
    for i in range(pairs // STEP):
        v = columns(cols_ref, (view,), i).astype(f32)
        total, squares = total + lanes(v), squares + lanes(v * v)
    return stats(jnp.sum(total, 1, keepdims=True), jnp.sum(squares, 1, keepdims=True), pairs)


def normalize(v, mean, inverse):
    return ((v.astype(f32) - mean) * inverse).astype(bf16)


def matmul(left, right):
    return jnp.dot(left, right, preferred_element_type=f32)


def grad_kernel(own_ref, other_ref, cols_ref, target_ref, grad_ref, stats_ref):
    pairs = cols_ref.shape[3]
    halves = (own_ref, other_ref)
    owned, width = grad_ref.shape
    mean, inverse = column_stats(halves, 0, pairs)
    mean_b, inverse_b = row_stats(cols_ref, 0, pairs)
    stats_ref[0:8, :] = jnp.broadcast_to(mean, (8, width))
    stats_ref[8:16, :] = jnp.broadcast_to(inverse, (8, width))
    corr = jnp.zeros((owned, width), f32)
    for i in range(pairs // STEP):
        v = normalize(chunk(halves, 0, i), mean, inverse)
        b = normalize(columns(cols_ref, (0,), i), mean_b, inverse_b)
        corr = corr + matmul(b, v)
    corr = corr / pairs
    diagonal = lax.broadcasted_iota(jnp.int32, (owned, width), 1) == target_ref[...]
    grad_ref[...] = jnp.where(diagonal, -2.0 * (1.0 - corr), 2.0 * off_weight * corr).astype(bf16)


def product_kernel(cols_ref, own_ref, other_ref, stats_ref, prod_ref, centered_ref, inverse_ref):
    pairs = cols_ref.shape[3]
    halves = (own_ref, other_ref)
    owned, width = prod_ref.shape[0], prod_ref.shape[1] // 2
    mean_a, inverse_a = stats_ref[0:1, :], stats_ref[8:9, :]
    mean_b, inverse_b = column_stats(halves, 1, pairs)
    inverse_ref[...] = jnp.broadcast_to(inverse_b, (8, width))
    prod_a = prod_b = jnp.zeros((owned, width), f32)
    sum_a = sum_b = jnp.zeros((8, width), f32)
    sum_h = jnp.zeros((owned, 128), f32)
    for i in range(pairs // STEP):
        h = columns(cols_ref, (0, 1), i)
        a = normalize(chunk(halves, 0, i), mean_a, inverse_a)
        b = normalize(chunk(halves, 1, i), mean_b, inverse_b)
        prod_a, prod_b = prod_a + matmul(h, a), prod_b + matmul(h, b)
        sum_a, sum_b = sum_a + fold(a.astype(f32)), sum_b + fold(b.astype(f32))
        sum_h = sum_h + lanes(h.astype(f32))
    sum_h = jnp.sum(sum_h, 1, keepdims=True)
    for side, prod, sums in ((0, prod_a, sum_a), (1, prod_b, sum_b)):
        cols = pl.ds(side * width, width)
        sums = jnp.sum(sums, 0, keepdims=True) / pairs
        prod_ref[:, cols] = prod
        centered_ref[:, cols] = (prod - sum_h * sums).astype(bf16)


def weight_a_kernel(pairs, blocks_ref, grads_ref, aa_ref, bb_ref, stats_ref, inverse_ref, second_ref, out_ref):
    owned, width = aa_ref.shape
    total = jnp.zeros((owned, width), f32)
    for x in range(blocks_ref.shape[0]):
        for zl in range(blocks_ref.shape[1]):
            total = total + matmul(blocks_ref[x, zl], grads_ref[x, zl])
    inv_b = inverse_ref[0:1, :]
    out_ref[0:owned, :] = stats_ref[8:9, :] * (total - pairs * aa_ref[...] * second_ref[...])
    out_ref[owned : 2 * owned, :] = inv_b * pairs * bb_ref[...]
    out_ref[2 * owned :, :] = jnp.broadcast_to(inv_b, (8, width))


def split(m, rows):
    high = m.astype(bf16)
    low = (m - high.astype(f32)).astype(bf16)
    pad = jnp.zeros((rows - 2 * m.shape[0], m.shape[1]), bf16)
    return jnp.concatenate([high, low, pad], axis=0)


def fold_kernel(width, got_ref, out_ref):
    count, blocks, _, owned = got_ref.shape
    rows = out_ref.shape[1]
    extra = width // owned
    for z in range(blocks):
        total = got_ref[0, z, 0:rows].astype(f32)
        for x in range(1, count):
            total = total + got_ref[x, z, 0:rows].astype(f32)
        out_ref[z, 0:width, :] = total[:width].astype(bf16)
        m = total[width : width + extra] + total[width + extra : width + 2 * extra]
        out_ref[z, width:rows, :] = split(m, rows - width)


def finish_kernel(got_ref, side_ref, out_ref):
    count, rows, owned = got_ref.shape
    width = side_ref.shape[1]
    extra = width // owned
    total = got_ref[0].astype(f32)
    for z in range(1, count):
        total = total + got_ref[z].astype(f32)
    m = total[width : width + extra] + total[width + extra : width + 2 * extra]
    second_b = jnp.concatenate([m[i : i + 1] for i in range(extra)], axis=1)
    w_b = total[:width].T
    inv_b = side_ref[2 * owned : 2 * owned + 1, :]
    result = side_ref[0:owned, :] + inv_b * w_b - side_ref[owned : 2 * owned, :] * second_b
    n_feat, sub, _ = out_ref.shape
    n_x = n_feat // count
    for x in range(n_x):
        for z in range(count):
            first = (x * count + z) * sub
            out_ref[z * n_x + x] = result[first : first + sub]


def call(kernel, name, flops, shapes, *operands):
    size = lambda v: v.size * v.dtype.itemsize
    outs = jax.tree.leaves(shapes)
    moved = sum(size(v) for v in operands) + sum(size(v) for v in outs)
    return pl.pallas_call(
        kernel,
        out_shape=shapes,
        in_specs=[pl.BlockSpec(memory_space=pltpu.VMEM)] * len(operands),
        out_specs=jax.tree.map(lambda _: pl.BlockSpec(memory_space=pltpu.VMEM), shapes),
        compiler_params=pltpu.CompilerParams(vmem_limit_bytes=16 * 2**20),
        cost_estimate=pl.CostEstimate(flops=flops, bytes_accessed=moved, transcendentals=0),
        name=name,
    )(*operands)


def body(h_a, h_b, z_a, z_b):
    local_rows, width = z_a.shape
    n_dp = lax.axis_size(DP)
    n_feat = lax.axis_size(FEAT)
    n_y, n_zh, n_c = (lax.axis_size(a) for a in DP)
    n_zl, n_x = (lax.axis_size(a) for a in FEAT)
    pairs = local_rows * n_dp
    sub = width // n_dp
    owned = n_feat * sub
    shape = jax.ShapeDtypeStruct
    together = lax.optimization_barrier

    core = lax.axis_index("c")

    def swap(v):
        return lax.ppermute(v, "c", [(0, 1), (1, 0)])

    with jax.named_scope("rows"):
        rows = collect(jnp.stack([z_a, z_b]), "zh")

    with jax.named_scope("columns"):
        cut = jnp.stack([v.T.reshape(n_dp, sub, local_rows) for v in (z_b, h_a, h_b)], axis=1)
        cut = lax.all_to_all(cut, DP, 0, 0, tiled=True)
        cut, rows = together((cut, rows))
        cut = cut.reshape(n_y, n_zh, n_c, 3, sub, local_rows)
        cut = jnp.where(core == 0, cut, jnp.flip(cut, 2))
        cut = cut.transpose(3, 4, 2, 0, 1, 5).reshape(3, sub, pairs)
        cut = collect(cut, "zl").transpose(1, 0, 2, 3).reshape(3, n_zl * sub, pairs)
        cols_b = gather(cut[:1], "x")
    with jax.named_scope("rows"):
        rows = collect(rows, "y")
    rows, cut, cols_b = together((rows, cut, cols_b))
    with jax.named_scope("columns"):
        cols_h = collect(cut[1:], "x")
    with jax.named_scope("rows"):
        own = rows.reshape(n_y * n_zh, 2, local_rows, width)
        other = swap(own)

    with jax.named_scope("grad"):
        f_index = lax.axis_index(FEAT)
        p_index = lax.axis_index(DP)
        row = lax.broadcasted_iota(jnp.int32, (owned, 1), 0)
        row_f = (row // sub % n_zl) * n_x + row // (sub * n_zl)
        target = jnp.where(row_f == f_index, p_index * sub + row % sub, -1)
        grad, stats_a = call(
            grad_kernel, "grad_block", 2 * pairs * owned * width,
            (shape((owned, width), bf16), shape((16, width), f32)),
            own, other, cols_b, target,
        )

    with jax.named_scope("grad_rows"):
        grads = collect(grad, "zh")
    own, _ = together((own, grads))

    with jax.named_scope("grad_rows"):
        grads = gather(grads, "y")
    with jax.named_scope("products"):
        prod, centered, inverse_b = call(
            product_kernel, "products", 8 * pairs * owned * width,
            (shape((2 * owned, 2 * width), f32), shape((2 * owned, 2 * width), bf16), shape((8, width), f32)),
            cols_h, own, other, stats_a,
        )
        halves = lambda v: v.reshape(n_x, 2, n_zl * sub, 2 * width)
        prod, centered = halves(prod), halves(centered)
        p_aa = prod[:, 0, :, :width].reshape(owned, width)
        p_bb = prod[:, 1, :, width:].reshape(owned, width)
        p_ab = centered[:, 0, :, width:].reshape(owned, width)
        p_ba = centered[:, 1, :, :width].reshape(owned, width)
        p_ab = collect(p_ab, "zl")
    grads, p_ab, p_ba = together((grads, p_ab, p_ba))
    with jax.named_scope("products"):
        p_ab = collect(p_ab, "x")

    with jax.named_scope("grad_rows"):
        grads = gather(grads, "c")
        grads = grads.reshape(n_c, n_y, n_zh, n_x, n_zl, sub, width)
        grads = grads.transpose(3, 4, 1, 2, 0, 5, 6).reshape(n_x, n_zl, width, width)
    with jax.named_scope("moments"):
        g = grads.astype(f32)
        four = lambda d: lax.broadcasted_iota(jnp.int32, g.shape, d)
        on = (four(1) * n_x + four(0) == f_index) & (four(2) == four(3))
        weighed = g * jnp.where(on, 1.0 + 0.5 * g, g * (0.5 / off_weight)) / pairs
        second_a = jnp.sum(weighed, (0, 1, 2))
        part_b = jnp.sum(weighed, 3)

    with jax.named_scope("weight_b"):
        flat = grads.reshape(n_feat * width, width)
        w_b = dot(flat, p_ba, ((1,), (1,))).astype(bf16).reshape(n_x, n_zl, width, owned)

        def with_moments(w, m):
            high = m.astype(bf16)
            low = (m - high.astype(f32)).astype(bf16)
            lead = m.shape[:-1]
            extra = jnp.concatenate(
                [high.reshape(*lead, -1, owned), low.reshape(*lead, -1, owned)], axis=-2
            )
            pad = jnp.zeros((*lead, 16 - extra.shape[-2], owned), bf16)
            return jnp.concatenate([w, extra, pad], axis=-2)

        got = lax.all_to_all(with_moments(w_b, part_b), "x", 0, 0, tiled=True)
        rows_out = got.shape[2]
        got = call(
            lambda *refs: fold_kernel(width, *refs), "fold", 0,
            shape((n_zl, rows_out, owned), bf16), got,
        )
        got = lax.all_to_all(got, "zl", 0, 0, tiled=True)

    with jax.named_scope("weight_a"):
        side = call(
            lambda *refs: weight_a_kernel(pairs, *refs), "weight_a", 2 * owned * n_feat * width * width,
            shape((2 * owned + 8, width), f32),
            p_ab, grads, p_aa, p_bb, stats_a, inverse_b, second_a[None],
        )

    with jax.named_scope("finish"):
        result = call(finish_kernel, "finish", 0, shape((n_feat, sub, width), f32), got, side)
        return result[:, None]


def solution(mesh):
    names = tuple(n for n, _ in SIZES)
    fine = Mesh(mesh.devices.reshape(tuple(s for _, s in SIZES)), names)
    spec = P(DP, FEAT)
    return jax.shard_map(
        body,
        mesh=fine,
        in_specs=(spec, spec, spec, spec),
        out_specs=P(None, DP, None, FEAT),
        check_vma=False,
    )
```

```python
import jax
import jax.numpy as jnp
from jax import lax
from jax.experimental import pallas as pl
from jax.experimental.pallas import tpu as pltpu
from jax.sharding import Mesh, PartitionSpec as P

epsilon = 1e-05
off_weight = 0.0051

SIZES = (("y", 4), ("zh", 4), ("c", 2), ("zl", 4), ("x", 4))
DP = ("y", "zh", "c")
FEAT = ("zl", "x")
bf16 = jnp.bfloat16
f32 = jnp.float32


def gather(block, axis):
    count = lax.axis_size(axis)
    copies = jnp.broadcast_to(block[None], (count, *block.shape))
    return lax.all_to_all(copies, axis, 0, 0, tiled=True)


def stats(total, squares, pair_count):
    mean = total / pair_count
    variance = squares / pair_count - mean * mean
    return mean, lax.rsqrt(variance + epsilon)


def dot(left, right, dims):
    return lax.dot_general(left, right, (dims, ((), ())), preferred_element_type=f32)


def collect(block, axis):
    return lax.all_gather(block, axis, axis=0, tiled=False)


STEP = 256


def fold(v):
    return jnp.sum(v.reshape(v.shape[0] // 8, 8, v.shape[1]), 0)


def lanes(v):
    return v[:, :128] + v[:, 128:]


def chunk(halves, side, i):
    own, other = halves
    count = own.shape[0] * own.shape[2] // STEP
    each = STEP // own.shape[2]
    ref = own if i < count else other
    first = (i % count) * each
    return jnp.concatenate([ref[first + j, side] for j in range(each)], axis=0)


def columns(cols_ref, views, i):
    at = pl.ds(i * STEP, STEP)
    return jnp.concatenate([cols_ref[x, v, :, at] for x in range(cols_ref.shape[0]) for v in views], axis=0)


def column_stats(halves, side, pairs):
    width = halves[0].shape[3]
    total = squares = jnp.zeros((8, width), f32)
    for i in range(pairs // STEP):
        v = chunk(halves, side, i).astype(f32)
        total, squares = total + fold(v), squares + fold(v * v)
    return stats(jnp.sum(total, 0, keepdims=True), jnp.sum(squares, 0, keepdims=True), pairs)


def row_stats(cols_ref, view, pairs):
    total = squares = 0.0
    for i in range(pairs // STEP):
        v = columns(cols_ref, (view,), i).astype(f32)
        total, squares = total + lanes(v), squares + lanes(v * v)
    return stats(jnp.sum(total, 1, keepdims=True), jnp.sum(squares, 1, keepdims=True), pairs)


def normalize(v, mean, inverse):
    return ((v.astype(f32) - mean) * inverse).astype(bf16)


def matmul(left, right):
    return jnp.dot(left, right, preferred_element_type=f32)


def open_kernel(z_a, z_b, h_a, h_b, rows_ref, cut_ref, held_a, held_b, sems):
    targets = (rows_ref.at[0], rows_ref.at[1], held_a, held_b)
    copies = [pltpu.make_async_copy(v, to, sems.at[i]) for i, (v, to) in enumerate(zip((z_a, z_b, h_a, h_b), targets))]
    for copy in copies:
        copy.start()
    copies[0].wait()
    for i, ref in enumerate((rows_ref.at[1], held_a, held_b)):
        copies[i + 1].wait()
        cut_ref[i] = ref[...].astype(f32).T.astype(bf16)


def grad_kernel(own_ref, other_ref, cols_ref, target_ref, grad_ref, stats_ref):
    pairs = cols_ref.shape[3]
    halves = (own_ref, other_ref)
    owned, width = grad_ref.shape
    mean, inverse = column_stats(halves, 0, pairs)
    mean_b, inverse_b = row_stats(cols_ref, 0, pairs)
    stats_ref[0:8, :] = jnp.broadcast_to(mean, (8, width))
    stats_ref[8:16, :] = jnp.broadcast_to(inverse, (8, width))
    corr = jnp.zeros((owned, width), f32)
    for i in range(pairs // STEP):
        v = normalize(chunk(halves, 0, i), mean, inverse)
        b = normalize(columns(cols_ref, (0,), i), mean_b, inverse_b)
        corr = corr + matmul(b, v)
    corr = corr / pairs
    diagonal = lax.broadcasted_iota(jnp.int32, (owned, width), 1) == target_ref[...]
    grad_ref[...] = jnp.where(diagonal, -2.0 * (1.0 - corr), 2.0 * off_weight * corr).astype(bf16)


def product_kernel(cols_ref, own_ref, other_ref, stats_ref, prod_ref, centered_ref, inverse_ref):
    pairs = cols_ref.shape[3]
    halves = (own_ref, other_ref)
    owned, width = prod_ref.shape[0], prod_ref.shape[1] // 2
    mean_a, inverse_a = stats_ref[0:1, :], stats_ref[8:9, :]
    mean_b, inverse_b = column_stats(halves, 1, pairs)
    inverse_ref[...] = jnp.broadcast_to(inverse_b, (8, width))
    prod_a = prod_b = jnp.zeros((owned, width), f32)
    sum_a = sum_b = jnp.zeros((8, width), f32)
    sum_h = jnp.zeros((owned, 128), f32)
    for i in range(pairs // STEP):
        h = columns(cols_ref, (0, 1), i)
        a = normalize(chunk(halves, 0, i), mean_a, inverse_a)
        b = normalize(chunk(halves, 1, i), mean_b, inverse_b)
        prod_a, prod_b = prod_a + matmul(h, a), prod_b + matmul(h, b)
        sum_a, sum_b = sum_a + fold(a.astype(f32)), sum_b + fold(b.astype(f32))
        sum_h = sum_h + lanes(h.astype(f32))
    sum_h = jnp.sum(sum_h, 1, keepdims=True)
    for side, prod, sums in ((0, prod_a, sum_a), (1, prod_b, sum_b)):
        cols = pl.ds(side * width, width)
        sums = jnp.sum(sums, 0, keepdims=True) / pairs
        prod_ref[:, cols] = prod
        centered_ref[:, cols] = (prod - sum_h * sums).astype(bf16)


def weight_a_kernel(pairs, blocks_ref, grads_ref, aa_ref, bb_ref, stats_ref, inverse_ref, second_ref, out_ref):
    owned, width = aa_ref.shape
    total = jnp.zeros((owned, width), f32)
    for x in range(blocks_ref.shape[0]):
        for zl in range(blocks_ref.shape[1]):
            total = total + matmul(blocks_ref[x, zl], grads_ref[x, zl])
    inv_b = inverse_ref[0:1, :]
    out_ref[0:owned, :] = stats_ref[8:9, :] * (total - pairs * aa_ref[...] * second_ref[...])
    out_ref[owned : 2 * owned, :] = inv_b * pairs * bb_ref[...]
    out_ref[2 * owned :, :] = jnp.broadcast_to(inv_b, (8, width))


def split(m, rows):
    high = m.astype(bf16)
    low = (m - high.astype(f32)).astype(bf16)
    pad = jnp.zeros((rows - 2 * m.shape[0], m.shape[1]), bf16)
    return jnp.concatenate([high, low, pad], axis=0)


def weight_b_kernel(pairs, block_ref, grads_ref, ba_ref, out_ref, second_ref):
    n_x, n_zl, width, _ = grads_ref.shape
    owned = ba_ref.shape[0]
    square = lambda axis: lax.broadcasted_iota(jnp.int32, (width, width), axis)
    on = square(0) == square(1)
    lane = lax.broadcasted_iota(jnp.int32, (width, owned), 1)
    second = jnp.zeros((8, width), f32)
    sums = jnp.zeros((width, owned), f32)
    for x in range(n_x):
        for z in range(n_zl):
            g = grads_ref[x, z]
            part = lax.dot_general(g, ba_ref[...], (((1,), (1,)), ((), ())), preferred_element_type=f32)
            out_ref[x, z, 0:width, :] = part.astype(bf16)
            g = g.astype(f32)
            diagonal = on & (block_ref[0] == x * n_zl + z)
            w = g * jnp.where(diagonal, 1.0 + 0.5 * g, g * (0.5 / off_weight)) / pairs
            second = second + fold(w)
            sums = sums + jnp.where(lane == x * n_zl + z, jnp.sum(w, 1, keepdims=True), 0.0)
    second_ref[...] = jnp.sum(second, 0, keepdims=True)
    sums = sums.T
    for x in range(n_x):
        for z in range(n_zl):
            row = sums[x * n_zl + z : x * n_zl + z + 1]
            row = jnp.concatenate([row[:, i : i + owned] for i in range(0, width, owned)], axis=0)
            out_ref[x, z, width:, :] = split(row, out_ref.shape[2] - width)


def fold_kernel(width, got_ref, out_ref):
    count, blocks, _, owned = got_ref.shape
    rows = out_ref.shape[1]
    extra = width // owned
    for z in range(blocks):
        total = got_ref[0, z, 0:rows].astype(f32)
        for x in range(1, count):
            total = total + got_ref[x, z, 0:rows].astype(f32)
        out_ref[z, 0:width, :] = total[:width].astype(bf16)
        m = total[width : width + extra] + total[width + extra : width + 2 * extra]
        out_ref[z, width:rows, :] = split(m, rows - width)


def finish_kernel(got_ref, side_ref, out_ref):
    count, rows, owned = got_ref.shape
    width = side_ref.shape[1]
    extra = width // owned
    total = got_ref[0].astype(f32)
    for z in range(1, count):
        total = total + got_ref[z].astype(f32)
    m = total[width : width + extra] + total[width + extra : width + 2 * extra]
    second_b = jnp.concatenate([m[i : i + 1] for i in range(extra)], axis=1)
    w_b = total[:width].T
    inv_b = side_ref[2 * owned : 2 * owned + 1, :]
    result = side_ref[0:owned, :] + inv_b * w_b - side_ref[owned : 2 * owned, :] * second_b
    n_feat, sub, _ = out_ref.shape
    n_x = n_feat // count
    for x in range(n_x):
        for z in range(count):
            first = (x * count + z) * sub
            out_ref[z * n_x + x] = result[first : first + sub]


def call(kernel, name, flops, shapes, *operands, scalars=0, hbm=False, scratch=(), grant=16):
    size = lambda v: v.size * v.dtype.itemsize
    outs = jax.tree.leaves(shapes)
    moved = sum(size(v) for v in operands) + sum(size(v) for v in outs)
    return pl.pallas_call(
        kernel,
        out_shape=shapes,
        scratch_shapes=list(scratch),
        in_specs=[
            pl.BlockSpec(memory_space=pltpu.SMEM if i < scalars else pl.ANY if hbm else pltpu.VMEM)
            for i in range(len(operands))
        ],
        out_specs=jax.tree.map(lambda _: pl.BlockSpec(memory_space=pltpu.VMEM), shapes),
        compiler_params=pltpu.CompilerParams(vmem_limit_bytes=grant * 2**20),
        cost_estimate=pl.CostEstimate(flops=flops, bytes_accessed=moved, transcendentals=0),
        name=name,
    )(*operands)


def body(h_a, h_b, z_a, z_b):
    local_rows, width = z_a.shape
    n_dp = lax.axis_size(DP)
    n_feat = lax.axis_size(FEAT)
    n_y, n_zh, n_c = (lax.axis_size(a) for a in DP)
    n_zl, n_x = (lax.axis_size(a) for a in FEAT)
    pairs = local_rows * n_dp
    sub = width // n_dp
    owned = n_feat * sub
    shape = jax.ShapeDtypeStruct
    together = lax.optimization_barrier

    core = lax.axis_index("c")

    def swap(v):
        return lax.ppermute(v, "c", [(0, 1), (1, 0)])

    with jax.named_scope("rows"):
        held = pltpu.VMEM((local_rows, width), bf16)
        rows, cut = call(
            open_kernel, "open", 0,
            (shape((2, local_rows, width), bf16), shape((3, width, local_rows), bf16)),
            z_a, z_b, h_a, h_b, hbm=True, grant=56,
            scratch=(held, held, pltpu.SemaphoreType.DMA((4,))),
        )
        rows = collect(rows, "zh")

    with jax.named_scope("columns"):
        cut = cut.reshape(3, n_dp, sub, local_rows).transpose(1, 0, 2, 3)
        cut = lax.all_to_all(cut, DP, 0, 0, tiled=True)
        cut, rows = together((cut, rows))
        cut = cut.reshape(n_y, n_zh, n_c, 3, sub, local_rows)
        cut = jnp.where(core == 0, cut, jnp.flip(cut, 2))
        cut = cut.transpose(3, 4, 2, 0, 1, 5).reshape(3, sub, pairs)
        cut = collect(cut, "zl").transpose(1, 0, 2, 3).reshape(3, n_zl * sub, pairs)
        cols_b = gather(cut[:1], "x")
    with jax.named_scope("rows"):
        rows = collect(rows, "y")
    rows, cut, cols_b = together((rows, cut, cols_b))
    with jax.named_scope("columns"):
        cols_h = collect(cut[1:], "x")
    with jax.named_scope("rows"):
        own = rows.reshape(n_y * n_zh, 2, local_rows, width)
        other = swap(own)

    with jax.named_scope("grad"):
        f_index = lax.axis_index(FEAT)
        p_index = lax.axis_index(DP)
        row = lax.broadcasted_iota(jnp.int32, (owned, 1), 0)
        row_f = (row // sub % n_zl) * n_x + row // (sub * n_zl)
        target = jnp.where(row_f == f_index, p_index * sub + row % sub, -1)
        grad, stats_a = call(
            grad_kernel, "grad_block", 2 * pairs * owned * width,
            (shape((owned, width), bf16), shape((16, width), f32)),
            own, other, cols_b, target,
        )

    with jax.named_scope("grad_rows"):
        grads = collect(grad, "zh")
    own, _ = together((own, grads))

    with jax.named_scope("grad_rows"):
        grads = gather(grads, "y")
    with jax.named_scope("products"):
        prod, centered, inverse_b = call(
            product_kernel, "products", 8 * pairs * owned * width,
            (shape((2 * owned, 2 * width), f32), shape((2 * owned, 2 * width), bf16), shape((8, width), f32)),
            cols_h, own, other, stats_a,
        )
        halves = lambda v: v.reshape(n_x, 2, n_zl * sub, 2 * width)
        prod, centered = halves(prod), halves(centered)
        p_aa = prod[:, 0, :, :width].reshape(owned, width)
        p_bb = prod[:, 1, :, width:].reshape(owned, width)
        p_ab = centered[:, 0, :, width:].reshape(owned, width)
        p_ba = centered[:, 1, :, :width].reshape(owned, width)
        p_ab = collect(p_ab, "zl")
    grads, p_ab, p_ba = together((grads, p_ab, p_ba))
    with jax.named_scope("products"):
        p_ab = collect(p_ab, "x")

    with jax.named_scope("grad_rows"):
        grads = gather(grads, "c")
        grads = grads.reshape(n_c, n_y, n_zh, n_x, n_zl, sub, width)
        grads = grads.transpose(3, 4, 1, 2, 0, 5, 6).reshape(n_x, n_zl, width, width)
    with jax.named_scope("weight_b"):
        block = (lax.axis_index("x") * n_zl + lax.axis_index("zl")).astype(jnp.int32)[None]
        got, second_a = call(
            lambda *refs: weight_b_kernel(pairs, *refs), "weight_b", 2 * owned * n_feat * width * width,
            (shape((n_x, n_zl, width + 16, owned), bf16), shape((1, width), f32)),
            block, grads, p_ba, scalars=1,
        )
        got = lax.all_to_all(got, "x", 0, 0, tiled=True)
        rows_out = got.shape[2]
        got = call(
            lambda *refs: fold_kernel(width, *refs), "fold", 0,
            shape((n_zl, rows_out, owned), bf16), got,
        )
        got = lax.all_to_all(got, "zl", 0, 0, tiled=True)

    with jax.named_scope("weight_a"):
        side = call(
            lambda *refs: weight_a_kernel(pairs, *refs), "weight_a", 2 * owned * n_feat * width * width,
            shape((2 * owned + 8, width), f32),
            p_ab, grads, p_aa, p_bb, stats_a, inverse_b, second_a,
        )

    with jax.named_scope("finish"):
        result = call(finish_kernel, "finish", 0, shape((n_feat, sub, width), f32), got, side)
        return result[:, None]


def solution(mesh):
    names = tuple(n for n, _ in SIZES)
    fine = Mesh(mesh.devices.reshape(tuple(s for _, s in SIZES)), names)
    spec = P(DP, FEAT)
    return jax.shard_map(
        body,
        mesh=fine,
        in_specs=(spec, spec, spec, spec),
        out_specs=P(None, DP, None, FEAT),
        check_vma=False,
    )
```

```python
import jax
import jax.numpy as jnp
from jax import lax
from jax.experimental import pallas as pl
from jax.experimental.pallas import tpu as pltpu
from jax.sharding import Mesh, PartitionSpec as P

epsilon = 1e-05
off_weight = 0.0051

SIZES = (("y", 4), ("zh", 4), ("c", 2), ("zl", 4), ("x", 4))
DP = ("y", "zh", "c")
FEAT = ("zl", "x")
bf16 = jnp.bfloat16
f32 = jnp.float32


def gather(block, axis):
    count = lax.axis_size(axis)
    copies = jnp.broadcast_to(block[None], (count, *block.shape))
    return lax.all_to_all(copies, axis, 0, 0, tiled=True)


def stats(total, squares, pair_count):
    mean = total / pair_count
    variance = squares / pair_count - mean * mean
    return mean, lax.rsqrt(variance + epsilon)


def dot(left, right, dims):
    return lax.dot_general(left, right, (dims, ((), ())), preferred_element_type=f32)


def collect(block, axis):
    return lax.all_gather(block, axis, axis=0, tiled=False)


STEP = 256


def fold(v):
    return jnp.sum(v.reshape(v.shape[0] // 8, 8, v.shape[1]), 0)


def lanes(v):
    return v[:, :128] + v[:, 128:]


def chunk(halves, side, i):
    own, other = halves
    count = own.shape[0] * own.shape[2] // STEP
    each = STEP // own.shape[2]
    ref = own if i < count else other
    first = (i % count) * each
    return jnp.concatenate([ref[first + j, side] for j in range(each)], axis=0)


def columns(cols_ref, views, i):
    at = pl.ds(i * STEP, STEP)
    return jnp.concatenate([cols_ref[x, v, :, at] for x in range(cols_ref.shape[0]) for v in views], axis=0)


def column_stats(halves, side, pairs):
    width = halves[0].shape[3]
    total = squares = jnp.zeros((8, width), f32)
    for i in range(pairs // STEP):
        v = chunk(halves, side, i).astype(f32)
        total, squares = total + fold(v), squares + fold(v * v)
    return stats(jnp.sum(total, 0, keepdims=True), jnp.sum(squares, 0, keepdims=True), pairs)


def row_stats(cols_ref, view, pairs):
    total = squares = 0.0
    for i in range(pairs // STEP):
        v = columns(cols_ref, (view,), i).astype(f32)
        total, squares = total + lanes(v), squares + lanes(v * v)
    return stats(jnp.sum(total, 1, keepdims=True), jnp.sum(squares, 1, keepdims=True), pairs)


def normalize(v, mean, inverse):
    return ((v.astype(f32) - mean) * inverse).astype(bf16)


def matmul(left, right):
    return jnp.dot(left, right, preferred_element_type=f32)


def open_kernel(z_a, z_b, h_a, h_b, rows_ref, cut_ref, held_a, held_b, sems):
    targets = (rows_ref.at[0], rows_ref.at[1], held_a, held_b)
    copies = [pltpu.make_async_copy(v, to, sems.at[i]) for i, (v, to) in enumerate(zip((z_a, z_b, h_a, h_b), targets))]
    for copy in copies:
        copy.start()
    copies[0].wait()
    for i, ref in enumerate((rows_ref.at[1], held_a, held_b)):
        copies[i + 1].wait()
        cut_ref[i] = ref[...].astype(f32).T.astype(bf16)


def grad_kernel(own_ref, other_ref, cols_ref, target_ref, grad_ref, stats_ref):
    pairs = cols_ref.shape[3]
    halves = (own_ref, other_ref)
    owned, width = grad_ref.shape
    mean, inverse = column_stats(halves, 0, pairs)
    mean_b, inverse_b = row_stats(cols_ref, 0, pairs)
    stats_ref[0:8, :] = jnp.broadcast_to(mean, (8, width))
    stats_ref[8:16, :] = jnp.broadcast_to(inverse, (8, width))
    corr = jnp.zeros((owned, width), f32)
    for i in range(pairs // STEP):
        v = normalize(chunk(halves, 0, i), mean, inverse)
        b = normalize(columns(cols_ref, (0,), i), mean_b, inverse_b)
        corr = corr + matmul(b, v)
    corr = corr / pairs
    diagonal = lax.broadcasted_iota(jnp.int32, (owned, width), 1) == target_ref[...]
    grad_ref[...] = jnp.where(diagonal, -2.0 * (1.0 - corr), 2.0 * off_weight * corr).astype(bf16)


def product_kernel(cols_ref, own_ref, other_ref, stats_ref, aa_ref, bb_ref, ab_ref, ba_ref, inverse_ref):
    pairs = cols_ref.shape[3]
    halves = (own_ref, other_ref)
    count, part = cols_ref.shape[0], cols_ref.shape[2]
    owned, width = 2 * aa_ref.shape[0], aa_ref.shape[1]
    mean_a, inverse_a = stats_ref[0:1, :], stats_ref[8:9, :]
    mean_b, inverse_b = column_stats(halves, 1, pairs)
    inverse_ref[...] = jnp.broadcast_to(inverse_b, (8, width))
    prod_a = prod_b = jnp.zeros((owned, width), f32)
    sum_a = sum_b = jnp.zeros((8, width), f32)
    sum_h = jnp.zeros((owned, 128), f32)
    for i in range(pairs // STEP):
        h = columns(cols_ref, (0, 1), i)
        a = normalize(chunk(halves, 0, i), mean_a, inverse_a)
        b = normalize(chunk(halves, 1, i), mean_b, inverse_b)
        prod_a, prod_b = prod_a + matmul(h, a), prod_b + matmul(h, b)
        sum_a, sum_b = sum_a + fold(a.astype(f32)), sum_b + fold(b.astype(f32))
        sum_h = sum_h + lanes(h.astype(f32))
    sum_h = jnp.sum(sum_h, 1, keepdims=True)
    for side, prod, sums, plain_ref, centered_ref in (
        (0, prod_a, sum_a, aa_ref, ba_ref),
        (1, prod_b, sum_b, bb_ref, ab_ref),
    ):
        centered = prod - sum_h * (jnp.sum(sums, 0, keepdims=True) / pairs)
        for x in range(count):
            block = lambda v, view: v[(2 * x + view) * part : (2 * x + view + 1) * part]
            plain_ref[x * part : (x + 1) * part, :] = block(prod, side)
            centered_ref[x * part : (x + 1) * part, :] = block(centered, 1 - side).astype(bf16)


def weight_a_kernel(pairs, blocks_ref, grads_ref, aa_ref, bb_ref, stats_ref, inverse_ref, second_ref, out_ref):
    owned, width = aa_ref.shape
    total = jnp.zeros((owned, width), f32)
    for x in range(blocks_ref.shape[0]):
        for zl in range(blocks_ref.shape[1]):
            total = total + matmul(blocks_ref[x, zl], grads_ref[x, zl])
    inv_b = inverse_ref[0:1, :]
    out_ref[0:owned, :] = stats_ref[8:9, :] * (total - pairs * aa_ref[...] * second_ref[...])
    out_ref[owned : 2 * owned, :] = inv_b * pairs * bb_ref[...]
    out_ref[2 * owned :, :] = jnp.broadcast_to(inv_b, (8, width))


def split(m, rows):
    high = m.astype(bf16)
    low = (m - high.astype(f32)).astype(bf16)
    pad = jnp.zeros((rows - 2 * m.shape[0], m.shape[1]), bf16)
    return jnp.concatenate([high, low, pad], axis=0)


def weight_b_kernel(pairs, block_ref, grads_ref, ba_ref, out_ref, second_ref):
    n_x, n_zl, width, _ = grads_ref.shape
    owned = ba_ref.shape[0]
    square = lambda axis: lax.broadcasted_iota(jnp.int32, (width, width), axis)
    on = square(0) == square(1)
    lane = lax.broadcasted_iota(jnp.int32, (width, owned), 1)
    second = jnp.zeros((8, width), f32)
    sums = jnp.zeros((width, owned), f32)
    for x in range(n_x):
        for z in range(n_zl):
            g = grads_ref[x, z]
            part = lax.dot_general(g, ba_ref[...], (((1,), (1,)), ((), ())), preferred_element_type=f32)
            out_ref[x, z, 0:width, :] = part.astype(bf16)
            g = g.astype(f32)
            diagonal = on & (block_ref[0] == x * n_zl + z)
            w = g * jnp.where(diagonal, 1.0 + 0.5 * g, g * (0.5 / off_weight)) / pairs
            second = second + fold(w)
            sums = sums + jnp.where(lane == x * n_zl + z, jnp.sum(w, 1, keepdims=True), 0.0)
    second_ref[...] = jnp.sum(second, 0, keepdims=True)
    sums = sums.T
    for x in range(n_x):
        for z in range(n_zl):
            row = sums[x * n_zl + z : x * n_zl + z + 1]
            row = jnp.concatenate([row[:, i : i + owned] for i in range(0, width, owned)], axis=0)
            out_ref[x, z, width:, :] = split(row, out_ref.shape[2] - width)


def fold_kernel(width, got_ref, out_ref):
    count, blocks, _, owned = got_ref.shape
    rows = out_ref.shape[1]
    extra = width // owned
    for z in range(blocks):
        total = got_ref[0, z, 0:rows].astype(f32)
        for x in range(1, count):
            total = total + got_ref[x, z, 0:rows].astype(f32)
        out_ref[z, 0:width, :] = total[:width].astype(bf16)
        m = total[width : width + extra] + total[width + extra : width + 2 * extra]
        out_ref[z, width:rows, :] = split(m, rows - width)


def finish_kernel(got_ref, side_ref, out_ref):
    count, rows, owned = got_ref.shape
    width = side_ref.shape[1]
    extra = width // owned
    total = got_ref[0].astype(f32)
    for z in range(1, count):
        total = total + got_ref[z].astype(f32)
    m = total[width : width + extra] + total[width + extra : width + 2 * extra]
    second_b = jnp.concatenate([m[i : i + 1] for i in range(extra)], axis=1)
    w_b = total[:width].T
    inv_b = side_ref[2 * owned : 2 * owned + 1, :]
    result = side_ref[0:owned, :] + inv_b * w_b - side_ref[owned : 2 * owned, :] * second_b
    n_feat, sub, _ = out_ref.shape
    n_x = n_feat // count
    for x in range(n_x):
        for z in range(count):
            first = (x * count + z) * sub
            out_ref[z * n_x + x] = result[first : first + sub]


def call(kernel, name, flops, shapes, *operands, scalars=0, hbm=False, scratch=(), grant=16):
    size = lambda v: v.size * v.dtype.itemsize
    outs = jax.tree.leaves(shapes)
    moved = sum(size(v) for v in operands) + sum(size(v) for v in outs)
    return pl.pallas_call(
        kernel,
        out_shape=shapes,
        scratch_shapes=list(scratch),
        in_specs=[
            pl.BlockSpec(memory_space=pltpu.SMEM if i < scalars else pl.ANY if hbm else pltpu.VMEM)
            for i in range(len(operands))
        ],
        out_specs=jax.tree.map(lambda _: pl.BlockSpec(memory_space=pltpu.VMEM), shapes),
        compiler_params=pltpu.CompilerParams(vmem_limit_bytes=grant * 2**20),
        cost_estimate=pl.CostEstimate(flops=flops, bytes_accessed=moved, transcendentals=0),
        name=name,
    )(*operands)


def body(h_a, h_b, z_a, z_b):
    local_rows, width = z_a.shape
    n_dp = lax.axis_size(DP)
    n_feat = lax.axis_size(FEAT)
    n_y, n_zh, n_c = (lax.axis_size(a) for a in DP)
    n_zl, n_x = (lax.axis_size(a) for a in FEAT)
    pairs = local_rows * n_dp
    sub = width // n_dp
    owned = n_feat * sub
    shape = jax.ShapeDtypeStruct
    together = lax.optimization_barrier

    core = lax.axis_index("c")

    def swap(v):
        return lax.ppermute(v, "c", [(0, 1), (1, 0)])

    with jax.named_scope("rows"):
        held = pltpu.VMEM((local_rows, width), bf16)
        rows, cut = call(
            open_kernel, "open", 0,
            (shape((2, local_rows, width), bf16), shape((3, width, local_rows), bf16)),
            z_a, z_b, h_a, h_b, hbm=True, grant=56,
            scratch=(held, held, pltpu.SemaphoreType.DMA((4,))),
        )
        rows = collect(rows, "zh")

    with jax.named_scope("columns"):
        cut = cut.reshape(3, n_dp, sub, local_rows).transpose(1, 0, 2, 3)
        cut = lax.all_to_all(cut, DP, 0, 0, tiled=True)
        cut, rows = together((cut, rows))
        cut = cut.reshape(n_y, n_zh, n_c, 3, sub, local_rows)
        cut = jnp.where(core == 0, cut, jnp.flip(cut, 2))
        cut = cut.transpose(3, 4, 2, 0, 1, 5).reshape(3, sub, pairs)
        cut = collect(cut, "zl").transpose(1, 0, 2, 3).reshape(3, n_zl * sub, pairs)
        cols_b = gather(cut[:1], "x")
    with jax.named_scope("rows"):
        rows = collect(rows, "y")
    rows, cut, cols_b = together((rows, cut, cols_b))
    with jax.named_scope("columns"):
        cols_h = collect(cut[1:], "x")
    with jax.named_scope("rows"):
        own = rows.reshape(n_y * n_zh, 2, local_rows, width)
        other = swap(own)

    with jax.named_scope("grad"):
        f_index = lax.axis_index(FEAT)
        p_index = lax.axis_index(DP)
        row = lax.broadcasted_iota(jnp.int32, (owned, 1), 0)
        row_f = (row // sub % n_zl) * n_x + row // (sub * n_zl)
        target = jnp.where(row_f == f_index, p_index * sub + row % sub, -1)
        grad, stats_a = call(
            grad_kernel, "grad_block", 2 * pairs * owned * width,
            (shape((owned, width), bf16), shape((16, width), f32)),
            own, other, cols_b, target,
        )

    with jax.named_scope("grad_rows"):
        grads = collect(grad, "zh")
    own, _ = together((own, grads))

    with jax.named_scope("grad_rows"):
        grads = gather(grads, "y")
    with jax.named_scope("products"):
        p_aa, p_bb, p_ab, p_ba, inverse_b = call(
            product_kernel, "products", 8 * pairs * owned * width,
            (shape((owned, width), f32),) * 2 + (shape((owned, width), bf16),) * 2 + (shape((8, width), f32),),
            cols_h, own, other, stats_a,
        )
        p_ab = collect(p_ab, "zl")
    grads, p_ab, p_ba = together((grads, p_ab, p_ba))
    with jax.named_scope("products"):
        p_ab = collect(p_ab, "x")

    with jax.named_scope("grad_rows"):
        grads = gather(grads, "c")
        grads = grads.reshape(n_c, n_y, n_zh, n_x, n_zl, sub, width)
        grads = grads.transpose(3, 4, 1, 2, 0, 5, 6).reshape(n_x, n_zl, width, width)
    with jax.named_scope("weight_b"):
        block = (lax.axis_index("x") * n_zl + lax.axis_index("zl")).astype(jnp.int32)[None]
        got, second_a = call(
            lambda *refs: weight_b_kernel(pairs, *refs), "weight_b", 2 * owned * n_feat * width * width,
            (shape((n_x, n_zl, width + 16, owned), bf16), shape((1, width), f32)),
            block, grads, p_ba, scalars=1,
        )
        got = lax.all_to_all(got, "x", 0, 0, tiled=True)
        rows_out = got.shape[2]
        got = call(
            lambda *refs: fold_kernel(width, *refs), "fold", 0,
            shape((n_zl, rows_out, owned), bf16), got,
        )
        got = lax.all_to_all(got, "zl", 0, 0, tiled=True)

    with jax.named_scope("weight_a"):
        side = call(
            lambda *refs: weight_a_kernel(pairs, *refs), "weight_a", 2 * owned * n_feat * width * width,
            shape((2 * owned + 8, width), f32),
            p_ab, grads, p_aa, p_bb, stats_a, inverse_b, second_a,
        )

    with jax.named_scope("finish"):
        result = call(finish_kernel, "finish", 0, shape((n_feat, sub, width), f32), got, side)
        return result[:, None]


def solution(mesh):
    names = tuple(n for n, _ in SIZES)
    fine = Mesh(mesh.devices.reshape(tuple(s for _, s in SIZES)), names)
    spec = P(DP, FEAT)
    return jax.shard_map(
        body,
        mesh=fine,
        in_specs=(spec, spec, spec, spec),
        out_specs=P(None, DP, None, FEAT),
        check_vma=False,
    )
```

```python
import jax
import jax.numpy as jnp
from jax import lax
from jax.experimental import pallas as pl
from jax.experimental.pallas import tpu as pltpu
from jax.sharding import Mesh, PartitionSpec as P

epsilon = 1e-05
off_weight = 0.0051

SIZES = (("y", 4), ("zh", 4), ("c", 2), ("zl", 4), ("x", 4))
DP = ("y", "zh", "c")
FEAT = ("zl", "x")
bf16 = jnp.bfloat16
f32 = jnp.float32


def gather(block, axis):
    count = lax.axis_size(axis)
    copies = jnp.broadcast_to(block[None], (count, *block.shape))
    return lax.all_to_all(copies, axis, 0, 0, tiled=True)


def stats(total, squares, pair_count):
    mean = total / pair_count
    variance = squares / pair_count - mean * mean
    return mean, lax.rsqrt(variance + epsilon)


def dot(left, right, dims):
    return lax.dot_general(left, right, (dims, ((), ())), preferred_element_type=f32)


def collect(block, axis):
    return lax.all_gather(block, axis, axis=0, tiled=False)


STEP = 256


def fold(v):
    return jnp.sum(v.reshape(v.shape[0] // 8, 8, v.shape[1]), 0)


def lanes(v):
    return v[:, :128] + v[:, 128:]


def chunk(halves, side, i):
    own, other = halves
    count = own.shape[0] * own.shape[2] // STEP
    each = STEP // own.shape[2]
    ref = own if i < count else other
    first = (i % count) * each
    return jnp.concatenate([ref[first + j, side] for j in range(each)], axis=0)


def columns(cols_ref, views, i):
    at = pl.ds(i * STEP, STEP)
    return jnp.concatenate([cols_ref[x, v, :, at] for x in range(cols_ref.shape[0]) for v in views], axis=0)


def column_stats(halves, side, pairs):
    width = halves[0].shape[3]
    total = squares = jnp.zeros((8, width), f32)
    for i in range(pairs // STEP):
        v = chunk(halves, side, i).astype(f32)
        total, squares = total + fold(v), squares + fold(v * v)
    return stats(jnp.sum(total, 0, keepdims=True), jnp.sum(squares, 0, keepdims=True), pairs)


def row_stats(cols_ref, view, pairs):
    total = squares = 0.0
    for i in range(pairs // STEP):
        v = columns(cols_ref, (view,), i).astype(f32)
        total, squares = total + lanes(v), squares + lanes(v * v)
    return stats(jnp.sum(total, 1, keepdims=True), jnp.sum(squares, 1, keepdims=True), pairs)


def normalize(v, mean, inverse):
    return ((v.astype(f32) - mean) * inverse).astype(bf16)


def matmul(left, right):
    return jnp.dot(left, right, preferred_element_type=f32)


def open_kernel(z_a, z_b, h_a, h_b, rows_ref, cut_ref, held_a, held_b, sems):
    targets = (rows_ref.at[0], rows_ref.at[1], held_a, held_b)
    copies = [pltpu.make_async_copy(v, to, sems.at[i]) for i, (v, to) in enumerate(zip((z_a, z_b, h_a, h_b), targets))]
    for copy in copies:
        copy.start()
    copies[0].wait()
    for i, ref in enumerate((rows_ref.at[1], held_a, held_b)):
        copies[i + 1].wait()
        cut_ref[i] = ref[...].astype(f32).T.astype(bf16)


def grad_kernel(own_ref, other_ref, cols_ref, target_ref, grad_ref, stats_ref):
    pairs = cols_ref.shape[3]
    halves = (own_ref, other_ref)
    owned, width = grad_ref.shape
    mean, inverse = column_stats(halves, 0, pairs)
    mean_b, inverse_b = row_stats(cols_ref, 0, pairs)
    stats_ref[0:8, :] = jnp.broadcast_to(mean, (8, width))
    stats_ref[8:16, :] = jnp.broadcast_to(inverse, (8, width))
    corr = jnp.zeros((owned, width), f32)
    for i in range(pairs // STEP):
        v = normalize(chunk(halves, 0, i), mean, inverse)
        b = normalize(columns(cols_ref, (0,), i), mean_b, inverse_b)
        corr = corr + matmul(b, v)
    corr = corr / pairs
    diagonal = lax.broadcasted_iota(jnp.int32, (owned, width), 1) == target_ref[...]
    grad_ref[...] = jnp.where(diagonal, -2.0 * (1.0 - corr), 2.0 * off_weight * corr).astype(bf16)


def product_kernel(cols_ref, own_ref, other_ref, stats_ref, plain_ref, ab_ref, ba_ref, inverse_ref):
    pairs = cols_ref.shape[3]
    halves = (own_ref, other_ref)
    count, part = cols_ref.shape[0], cols_ref.shape[2]
    owned, width = 2 * ab_ref.shape[0], ab_ref.shape[1]
    mean_a, inverse_a = stats_ref[0:1, :], stats_ref[8:9, :]
    mean_b, inverse_b = column_stats(halves, 1, pairs)
    inverse_ref[...] = jnp.broadcast_to(inverse_b, (8, width))
    prod_a = prod_b = jnp.zeros((owned, width), f32)
    sum_a = sum_b = jnp.zeros((8, width), f32)
    sum_h = jnp.zeros((owned, 128), f32)
    for i in range(pairs // STEP):
        h = columns(cols_ref, (0, 1), i)
        a = normalize(chunk(halves, 0, i), mean_a, inverse_a)
        b = normalize(chunk(halves, 1, i), mean_b, inverse_b)
        prod_a, prod_b = prod_a + matmul(h, a), prod_b + matmul(h, b)
        sum_a, sum_b = sum_a + fold(a.astype(f32)), sum_b + fold(b.astype(f32))
        sum_h = sum_h + lanes(h.astype(f32))
    sum_h = jnp.sum(sum_h, 1, keepdims=True)
    for side, prod, sums, centered_ref in (
        (0, prod_a, sum_a, ba_ref),
        (1, prod_b, sum_b, ab_ref),
    ):
        centered = prod - sum_h * (jnp.sum(sums, 0, keepdims=True) / pairs)
        for x in range(count):
            block = lambda v, view: v[(2 * x + view) * part : (2 * x + view + 1) * part]
            plain_ref[side, x * part : (x + 1) * part, :] = block(prod, side)
            centered_ref[x * part : (x + 1) * part, :] = block(centered, 1 - side).astype(bf16)


def weight_a_kernel(pairs, x_ref, *refs):
    blocks, (grads_ref, plain_ref, stats_ref, inverse_ref, second_ref, out_ref) = refs[:-6], refs[-6:]
    _, owned, width = plain_ref.shape
    total = jnp.zeros((owned, width), f32)
    for r, block in enumerate(blocks):
        x = lax.rem(x_ref[0] - r + len(blocks), len(blocks))
        for zl in range(block.shape[0]):
            total = total + matmul(block[zl], grads_ref[x, zl])
    inv_b = inverse_ref[0:1, :]
    out_ref[0:owned, :] = stats_ref[8:9, :] * (total - pairs * plain_ref[0] * second_ref[...])
    out_ref[owned : 2 * owned, :] = inv_b * pairs * plain_ref[1]
    out_ref[2 * owned :, :] = jnp.broadcast_to(inv_b, (8, width))


def split(m, rows):
    high = m.astype(bf16)
    low = (m - high.astype(f32)).astype(bf16)
    pad = jnp.zeros((rows - 2 * m.shape[0], m.shape[1]), bf16)
    return jnp.concatenate([high, low, pad], axis=0)


def weight_b_kernel(pairs, block_ref, grads_ref, ba_ref, out_ref, second_ref):
    n_x, n_zl, width, _ = grads_ref.shape
    owned = ba_ref.shape[0]
    square = lambda axis: lax.broadcasted_iota(jnp.int32, (width, width), axis)
    on = square(0) == square(1)
    lane = lax.broadcasted_iota(jnp.int32, (width, owned), 1)
    second = jnp.zeros((8, width), f32)
    sums = jnp.zeros((width, owned), f32)
    for x in range(n_x):
        for z in range(n_zl):
            g = grads_ref[x, z]
            part = lax.dot_general(g, ba_ref[...], (((1,), (1,)), ((), ())), preferred_element_type=f32)
            out_ref[x, z, 0:width, :] = part.astype(bf16)
            g = g.astype(f32)
            diagonal = on & (block_ref[0] == x * n_zl + z)
            w = g * jnp.where(diagonal, 1.0 + 0.5 * g, g * (0.5 / off_weight)) / pairs
            second = second + fold(w)
            sums = sums + jnp.where(lane == x * n_zl + z, jnp.sum(w, 1, keepdims=True), 0.0)
    second_ref[...] = jnp.sum(second, 0, keepdims=True)
    sums = sums.T
    for x in range(n_x):
        for z in range(n_zl):
            row = sums[x * n_zl + z : x * n_zl + z + 1]
            row = jnp.concatenate([row[:, i : i + owned] for i in range(0, width, owned)], axis=0)
            out_ref[x, z, width:, :] = split(row, out_ref.shape[2] - width)


def fold_kernel(width, got_ref, out_ref):
    count, blocks, _, owned = got_ref.shape
    rows = out_ref.shape[1]
    extra = width // owned
    for z in range(blocks):
        total = got_ref[0, z, 0:rows].astype(f32)
        for x in range(1, count):
            total = total + got_ref[x, z, 0:rows].astype(f32)
        out_ref[z, 0:width, :] = total[:width].astype(bf16)
        m = total[width : width + extra] + total[width + extra : width + 2 * extra]
        out_ref[z, width:rows, :] = split(m, rows - width)


def finish_kernel(got_ref, side_ref, out_ref):
    count, rows, owned = got_ref.shape
    width = side_ref.shape[1]
    extra = width // owned
    total = got_ref[0].astype(f32)
    for z in range(1, count):
        total = total + got_ref[z].astype(f32)
    m = total[width : width + extra] + total[width + extra : width + 2 * extra]
    second_b = jnp.concatenate([m[i : i + 1] for i in range(extra)], axis=1)
    w_b = total[:width].T
    inv_b = side_ref[2 * owned : 2 * owned + 1, :]
    result = side_ref[0:owned, :] + inv_b * w_b - side_ref[owned : 2 * owned, :] * second_b
    n_feat, sub, _ = out_ref.shape
    n_x = n_feat // count
    for x in range(n_x):
        for z in range(count):
            first = (x * count + z) * sub
            out_ref[z * n_x + x] = result[first : first + sub]


def call(kernel, name, flops, shapes, *operands, scalars=0, hbm=False, scratch=(), grant=16):
    size = lambda v: v.size * v.dtype.itemsize
    outs = jax.tree.leaves(shapes)
    moved = sum(size(v) for v in operands) + sum(size(v) for v in outs)
    return pl.pallas_call(
        kernel,
        out_shape=shapes,
        scratch_shapes=list(scratch),
        in_specs=[
            pl.BlockSpec(memory_space=pltpu.SMEM if i < scalars else pl.ANY if hbm else pltpu.VMEM)
            for i in range(len(operands))
        ],
        out_specs=jax.tree.map(lambda _: pl.BlockSpec(memory_space=pltpu.VMEM), shapes),
        compiler_params=pltpu.CompilerParams(vmem_limit_bytes=grant * 2**20),
        cost_estimate=pl.CostEstimate(flops=flops, bytes_accessed=moved, transcendentals=0),
        name=name,
    )(*operands)


def body(h_a, h_b, z_a, z_b):
    local_rows, width = z_a.shape
    n_dp = lax.axis_size(DP)
    n_feat = lax.axis_size(FEAT)
    n_y, n_zh, n_c = (lax.axis_size(a) for a in DP)
    n_zl, n_x = (lax.axis_size(a) for a in FEAT)
    pairs = local_rows * n_dp
    sub = width // n_dp
    owned = n_feat * sub
    shape = jax.ShapeDtypeStruct
    together = lax.optimization_barrier

    core = lax.axis_index("c")
    x_index = lax.axis_index("x").astype(jnp.int32)[None]

    def swap(v):
        return lax.ppermute(v, "c", [(0, 1), (1, 0)])

    with jax.named_scope("rows"):
        held = pltpu.VMEM((local_rows, width), bf16)
        rows, cut = call(
            open_kernel, "open", 0,
            (shape((2, local_rows, width), bf16), shape((3, width, local_rows), bf16)),
            z_a, z_b, h_a, h_b, hbm=True, grant=56,
            scratch=(held, held, pltpu.SemaphoreType.DMA((4,))),
        )
        rows = collect(rows, "zh")

    with jax.named_scope("columns"):
        cut = cut.reshape(3, n_dp, sub, local_rows).transpose(1, 0, 2, 3)
        cut = lax.all_to_all(cut, DP, 0, 0, tiled=True)
        cut, rows = together((cut, rows))
        cut = cut.reshape(n_y, n_zh, n_c, 3, sub, local_rows)
        cut = jnp.where(core == 0, cut, jnp.flip(cut, 2))
        cut = cut.transpose(3, 4, 2, 0, 1, 5).reshape(3, sub, pairs)
        cut = collect(cut, "zl").transpose(1, 0, 2, 3).reshape(3, n_zl * sub, pairs)
        cols_b = gather(cut[:1], "x")
    with jax.named_scope("rows"):
        rows = collect(rows, "y")
    rows, cut, cols_b = together((rows, cut, cols_b))
    with jax.named_scope("columns"):
        cols_h = collect(cut[1:], "x")
    with jax.named_scope("rows"):
        own = rows.reshape(n_y * n_zh, 2, local_rows, width)
        other = swap(own)

    with jax.named_scope("grad"):
        f_index = lax.axis_index(FEAT)
        p_index = lax.axis_index(DP)
        row = lax.broadcasted_iota(jnp.int32, (owned, 1), 0)
        row_f = (row // sub % n_zl) * n_x + row // (sub * n_zl)
        target = jnp.where(row_f == f_index, p_index * sub + row % sub, -1)
        grad, stats_a = call(
            grad_kernel, "grad_block", 2 * pairs * owned * width,
            (shape((owned, width), bf16), shape((16, width), f32)),
            own, other, cols_b, target,
        )

    with jax.named_scope("grad_rows"):
        grads = collect(grad, "zh")
    own, _ = together((own, grads))

    with jax.named_scope("grad_rows"):
        grads = gather(grads, "y")
    with jax.named_scope("products"):
        plain, p_ab, p_ba, inverse_b = call(
            product_kernel, "products", 8 * pairs * owned * width,
            (shape((2, owned, width), f32),) + (shape((owned, width), bf16),) * 2 + (shape((8, width), f32),),
            cols_h, own, other, stats_a,
        )
    grads, p_ab, p_ba = together((grads, p_ab, p_ba))
    with jax.named_scope("grad_rows"):
        grads = gather(grads, "c")
        grads = grads.reshape(n_c, n_y, n_zh, n_x, n_zl, sub, width)
        grads = grads.transpose(3, 4, 1, 2, 0, 5, 6).reshape(n_x, n_zl, width, width)
    with jax.named_scope("weight_b"):
        block = (lax.axis_index("x") * n_zl + lax.axis_index("zl")).astype(jnp.int32)[None]
        got, second_a = call(
            lambda *refs: weight_b_kernel(pairs, *refs), "weight_b", 2 * owned * n_feat * width * width,
            (shape((n_x, n_zl, width + 16, owned), bf16), shape((1, width), f32)),
            block, grads, p_ba, scalars=1,
        )
        got, p_ab = together((got, p_ab))
        got = lax.all_to_all(got, "x", 0, 0, tiled=True)
        p_ab = collect(p_ab, "zl")
        got, p_ab = together((got, p_ab))
        rows_out = got.shape[2]
        got = call(
            lambda *refs: fold_kernel(width, *refs), "fold", 0,
            shape((n_zl, rows_out, owned), bf16), got,
        )
        got = lax.all_to_all(got, "zl", 0, 0, tiled=True)
        turn = lambda r: [(i, (i + r) % n_x) for i in range(n_x)]
        p_ab = [p_ab] + [lax.ppermute(p_ab, "x", turn(r)) for r in range(1, n_x)]

    with jax.named_scope("weight_a"):
        side = call(
            lambda *refs: weight_a_kernel(pairs, *refs), "weight_a", 2 * owned * n_feat * width * width,
            shape((2 * owned + 8, width), f32),
            x_index, *p_ab, grads, plain, stats_a, inverse_b, second_a, scalars=1,
        )

    with jax.named_scope("finish"):
        result = call(finish_kernel, "finish", 0, shape((n_feat, sub, width), f32), got, side)
        return result[:, None]


def solution(mesh):
    names = tuple(n for n, _ in SIZES)
    fine = Mesh(mesh.devices.reshape(tuple(s for _, s in SIZES)), names)
    spec = P(DP, FEAT)
    return jax.shard_map(
        body,
        mesh=fine,
        in_specs=(spec, spec, spec, spec),
        out_specs=P(None, DP, None, FEAT),
        check_vma=False,
    )
```

```python
import jax
import jax.numpy as jnp
from jax import lax
from jax.experimental import pallas as pl
from jax.experimental.pallas import tpu as pltpu
from jax.sharding import Mesh, PartitionSpec as P

epsilon = 1e-05
off_weight = 0.0051

SIZES = (("y", 4), ("zh", 4), ("c", 2), ("zl", 4), ("x", 4))
DP = ("y", "zh", "c")
FEAT = ("zl", "x")
bf16 = jnp.bfloat16
f32 = jnp.float32


def gather(block, axis):
    count = lax.axis_size(axis)
    copies = jnp.broadcast_to(block[None], (count, *block.shape))
    return lax.all_to_all(copies, axis, 0, 0, tiled=True)


def stats(total, squares, pair_count):
    mean = total / pair_count
    variance = squares / pair_count - mean * mean
    return mean, lax.rsqrt(variance + epsilon)


def dot(left, right, dims):
    return lax.dot_general(left, right, (dims, ((), ())), preferred_element_type=f32)


def collect(block, axis):
    return lax.all_gather(block, axis, axis=0, tiled=False)


STEP = 256


def fold(v):
    return jnp.sum(v.reshape(v.shape[0] // 8, 8, v.shape[1]), 0)


def lanes(v):
    return v[:, :128] + v[:, 128:]


def chunk(halves, side, i):
    own, other = halves
    count = own.shape[0] * own.shape[2] // STEP
    each = STEP // own.shape[2]
    ref = own if i < count else other
    first = (i % count) * each
    return jnp.concatenate([ref[first + j, side] for j in range(each)], axis=0)


def columns(cols_ref, views, i):
    at = pl.ds(i * STEP, STEP)
    return jnp.concatenate([cols_ref[x, v, :, at] for x in range(cols_ref.shape[0]) for v in views], axis=0)


def column_stats(halves, side, pairs):
    width = halves[0].shape[3]
    total = squares = jnp.zeros((8, width), f32)
    for i in range(pairs // STEP):
        v = chunk(halves, side, i).astype(f32)
        total, squares = total + fold(v), squares + fold(v * v)
    return stats(jnp.sum(total, 0, keepdims=True), jnp.sum(squares, 0, keepdims=True), pairs)


def row_stats(cols_ref, view, pairs):
    total = squares = 0.0
    for i in range(pairs // STEP):
        v = columns(cols_ref, (view,), i).astype(f32)
        total, squares = total + lanes(v), squares + lanes(v * v)
    return stats(jnp.sum(total, 1, keepdims=True), jnp.sum(squares, 1, keepdims=True), pairs)


def normalize(v, mean, inverse):
    return ((v.astype(f32) - mean) * inverse).astype(bf16)


def matmul(left, right):
    return jnp.dot(left, right, preferred_element_type=f32)


def open_kernel(z_a, z_b, h_a, h_b, rows_ref, cut_ref, held_a, held_b, sems):
    targets = (rows_ref.at[0], rows_ref.at[1], held_a, held_b)
    copies = [pltpu.make_async_copy(v, to, sems.at[i]) for i, (v, to) in enumerate(zip((z_a, z_b, h_a, h_b), targets))]
    for copy in copies:
        copy.start()
    copies[0].wait()
    for i, ref in enumerate((rows_ref.at[1], held_a, held_b)):
        copies[i + 1].wait()
        cut_ref[i] = ref[...].astype(f32).T.astype(bf16)


def grad_kernel(own_ref, other_ref, cols_ref, target_ref, grad_ref, stats_ref):
    pairs = cols_ref.shape[3]
    halves = (own_ref, other_ref)
    owned, width = grad_ref.shape
    mean, inverse = column_stats(halves, 0, pairs)
    mean_b, inverse_b = row_stats(cols_ref, 0, pairs)
    stats_ref[0:8, :] = jnp.broadcast_to(mean, (8, width))
    stats_ref[8:16, :] = jnp.broadcast_to(inverse, (8, width))
    corr = jnp.zeros((owned, width), f32)
    for i in range(pairs // STEP):
        v = normalize(chunk(halves, 0, i), mean, inverse)
        b = normalize(columns(cols_ref, (0,), i), mean_b, inverse_b)
        corr = corr + matmul(b, v)
    corr = corr / pairs
    diagonal = lax.broadcasted_iota(jnp.int32, (owned, width), 1) == target_ref[...]
    grad_ref[...] = jnp.where(diagonal, -2.0 * (1.0 - corr), 2.0 * off_weight * corr).astype(bf16)


def product_kernel(cols_ref, own_ref, other_ref, stats_ref, plain_ref, ab_ref, ba_ref, inverse_ref):
    pairs = cols_ref.shape[3]
    halves = (own_ref, other_ref)
    count, part = cols_ref.shape[0], cols_ref.shape[2]
    owned, width = 2 * ab_ref.shape[0], ab_ref.shape[1]
    mean_a, inverse_a = stats_ref[0:1, :], stats_ref[8:9, :]
    mean_b, inverse_b = column_stats(halves, 1, pairs)
    inverse_ref[0:8, :] = jnp.broadcast_to(inverse_a, (8, width))
    inverse_ref[8:16, :] = jnp.broadcast_to(inverse_b, (8, width))
    prod_a = prod_b = jnp.zeros((owned, width), f32)
    sum_a = sum_b = jnp.zeros((8, width), f32)
    sum_h = jnp.zeros((owned, 128), f32)
    for i in range(pairs // STEP):
        h = columns(cols_ref, (0, 1), i)
        a = normalize(chunk(halves, 0, i), mean_a, inverse_a)
        b = normalize(chunk(halves, 1, i), mean_b, inverse_b)
        prod_a, prod_b = prod_a + matmul(h, a), prod_b + matmul(h, b)
        sum_a, sum_b = sum_a + fold(a.astype(f32)), sum_b + fold(b.astype(f32))
        sum_h = sum_h + lanes(h.astype(f32))
    sum_h = jnp.sum(sum_h, 1, keepdims=True)
    for side, prod, sums, centered_ref in (
        (0, prod_a, sum_a, ba_ref),
        (1, prod_b, sum_b, ab_ref),
    ):
        centered = prod - sum_h * (jnp.sum(sums, 0, keepdims=True) / pairs)
        for x in range(count):
            block = lambda v, view: v[(2 * x + view) * part : (2 * x + view + 1) * part]
            plain_ref[side, x * part : (x + 1) * part, :] = block(prod, side)
            centered_ref[x * part : (x + 1) * part, :] = block(centered, 1 - side).astype(bf16)


def weight_a_kernel(pairs, x_ref, *refs):
    blocks, (grads_ref, plain_ref, inverse_ref, second_ref, out_ref) = refs[:-5], refs[-5:]
    _, owned, width = plain_ref.shape
    total = jnp.zeros((owned, width), f32)
    for r, block in enumerate(blocks):
        x = lax.rem(x_ref[0] - r + len(blocks), len(blocks))
        for zl in range(block.shape[0]):
            total = total + matmul(block[zl], grads_ref[x, zl])
    inv_b = inverse_ref[8:9, :]
    out_ref[0:owned, :] = inverse_ref[0:1, :] * (total - pairs * plain_ref[0] * second_ref[...])
    out_ref[owned : 2 * owned, :] = inv_b * pairs * plain_ref[1]
    out_ref[2 * owned :, :] = jnp.broadcast_to(inv_b, (8, width))


def split(m, rows):
    high = m.astype(bf16)
    low = (m - high.astype(f32)).astype(bf16)
    pad = jnp.zeros((rows - 2 * m.shape[0], m.shape[1]), bf16)
    return jnp.concatenate([high, low, pad], axis=0)


def weight_b_kernel(pairs, block_ref, grads_ref, ba_ref, out_ref, second_ref):
    n_x, n_zl, width, _ = grads_ref.shape
    owned = ba_ref.shape[0]
    square = lambda axis: lax.broadcasted_iota(jnp.int32, (width, width), axis)
    on = square(0) == square(1)
    lane = lax.broadcasted_iota(jnp.int32, (width, owned), 1)
    second = jnp.zeros((8, width), f32)
    sums = jnp.zeros((width, owned), f32)
    for x in range(n_x):
        for z in range(n_zl):
            g = grads_ref[x, z]
            part = lax.dot_general(g, ba_ref[...], (((1,), (1,)), ((), ())), preferred_element_type=f32)
            out_ref[x, z, 0:width, :] = part.astype(bf16)
            g = g.astype(f32)
            diagonal = on & (block_ref[0] == x * n_zl + z)
            w = g * jnp.where(diagonal, 1.0 + 0.5 * g, g * (0.5 / off_weight)) / pairs
            second = second + fold(w)
            sums = sums + jnp.where(lane == x * n_zl + z, jnp.sum(w, 1, keepdims=True), 0.0)
    second_ref[...] = jnp.sum(second, 0, keepdims=True)
    sums = sums.T
    for x in range(n_x):
        for z in range(n_zl):
            row = sums[x * n_zl + z : x * n_zl + z + 1]
            row = jnp.concatenate([row[:, i : i + owned] for i in range(0, width, owned)], axis=0)
            out_ref[x, z, width:, :] = split(row, out_ref.shape[2] - width)


def fold_kernel(width, got_ref, out_ref):
    count, blocks, _, owned = got_ref.shape
    rows = out_ref.shape[1]
    extra = width // owned
    for z in range(blocks):
        total = got_ref[0, z, 0:rows].astype(f32)
        for x in range(1, count):
            total = total + got_ref[x, z, 0:rows].astype(f32)
        out_ref[z, 0:width, :] = total[:width].astype(bf16)
        m = total[width : width + extra] + total[width + extra : width + 2 * extra]
        out_ref[z, width:rows, :] = split(m, rows - width)


def finish_kernel(got_ref, side_ref, out_ref):
    count, rows, owned = got_ref.shape
    width = side_ref.shape[1]
    extra = width // owned
    total = got_ref[0].astype(f32)
    for z in range(1, count):
        total = total + got_ref[z].astype(f32)
    m = total[width : width + extra] + total[width + extra : width + 2 * extra]
    second_b = jnp.concatenate([m[i : i + 1] for i in range(extra)], axis=1)
    w_b = total[:width].T
    inv_b = side_ref[2 * owned : 2 * owned + 1, :]
    result = side_ref[0:owned, :] + inv_b * w_b - side_ref[owned : 2 * owned, :] * second_b
    n_feat, sub, _ = out_ref.shape
    n_x = n_feat // count
    for x in range(n_x):
        for z in range(count):
            first = (x * count + z) * sub
            out_ref[z * n_x + x] = result[first : first + sub]


def call(kernel, name, flops, shapes, *operands, scalars=0, hbm=False, scratch=(), grant=16):
    size = lambda v: v.size * v.dtype.itemsize
    outs = jax.tree.leaves(shapes)
    moved = sum(size(v) for v in operands) + sum(size(v) for v in outs)
    return pl.pallas_call(
        kernel,
        out_shape=shapes,
        scratch_shapes=list(scratch),
        in_specs=[
            pl.BlockSpec(memory_space=pltpu.SMEM if i < scalars else pl.ANY if hbm else pltpu.VMEM)
            for i in range(len(operands))
        ],
        out_specs=jax.tree.map(lambda _: pl.BlockSpec(memory_space=pltpu.VMEM), shapes),
        compiler_params=pltpu.CompilerParams(vmem_limit_bytes=grant * 2**20),
        cost_estimate=pl.CostEstimate(flops=flops, bytes_accessed=moved, transcendentals=0),
        name=name,
    )(*operands)


def body(h_a, h_b, z_a, z_b):
    local_rows, width = z_a.shape
    n_dp = lax.axis_size(DP)
    n_feat = lax.axis_size(FEAT)
    n_y, n_zh, n_c = (lax.axis_size(a) for a in DP)
    n_zl, n_x = (lax.axis_size(a) for a in FEAT)
    pairs = local_rows * n_dp
    sub = width // n_dp
    owned = n_feat * sub
    shape = jax.ShapeDtypeStruct
    together = lax.optimization_barrier

    core = lax.axis_index("c")
    x_index = lax.axis_index("x").astype(jnp.int32)[None]

    def swap(v):
        return lax.ppermute(v, "c", [(0, 1), (1, 0)])

    with jax.named_scope("rows"):
        held = pltpu.VMEM((local_rows, width), bf16)
        rows, cut = call(
            open_kernel, "open", 0,
            (shape((2, local_rows, width), bf16), shape((3, width, local_rows), bf16)),
            z_a, z_b, h_a, h_b, hbm=True, grant=56,
            scratch=(held, held, pltpu.SemaphoreType.DMA((4,))),
        )
        rows = collect(rows, "zh")

    with jax.named_scope("columns"):
        cut = cut.reshape(3, n_dp, sub, local_rows).transpose(1, 0, 2, 3)
        cut = lax.all_to_all(cut, DP, 0, 0, tiled=True)
        cut, rows = together((cut, rows))
        cut = cut.reshape(n_y, n_zh, n_c, 3, sub, local_rows)
        cut = jnp.where(core == 0, cut, jnp.flip(cut, 2))
        cut = cut.transpose(3, 4, 2, 0, 1, 5).reshape(3, sub, pairs)
        cut = collect(cut, "zl").transpose(1, 0, 2, 3).reshape(3, n_zl * sub, pairs)
        cols_b = gather(cut[:1], "x")
    with jax.named_scope("rows"):
        rows = collect(rows, "y")
    rows, cut, cols_b = together((rows, cut, cols_b))
    with jax.named_scope("columns"):
        cols_h = collect(cut[1:], "x")
    with jax.named_scope("rows"):
        own = rows.reshape(n_y * n_zh, 2, local_rows, width)
        other = swap(own)

    with jax.named_scope("grad"):
        f_index = lax.axis_index(FEAT)
        p_index = lax.axis_index(DP)
        row = lax.broadcasted_iota(jnp.int32, (owned, 1), 0)
        row_f = (row // sub % n_zl) * n_x + row // (sub * n_zl)
        target = jnp.where(row_f == f_index, p_index * sub + row % sub, -1)
        grad, stats_a = call(
            grad_kernel, "grad_block", 2 * pairs * owned * width,
            (shape((owned, width), bf16), shape((16, width), f32)),
            own, other, cols_b, target,
        )

    with jax.named_scope("grad_rows"):
        grads = collect(grad, "zh")
    own, _ = together((own, grads))

    with jax.named_scope("grad_rows"):
        grads = gather(grads, "y")
    with jax.named_scope("products"):
        plain, p_ab, p_ba, inverse = call(
            product_kernel, "products", 8 * pairs * owned * width,
            (shape((2, owned, width), f32),) + (shape((owned, width), bf16),) * 2 + (shape((16, width), f32),),
            cols_h, own, other, stats_a,
        )
    grads, p_ab, p_ba = together((grads, p_ab, p_ba))
    with jax.named_scope("grad_rows"):
        grads = gather(grads, "c")
        grads = grads.reshape(n_c, n_y, n_zh, n_x, n_zl, sub, width)
        grads = grads.transpose(3, 4, 1, 2, 0, 5, 6).reshape(n_x, n_zl, width, width)
    with jax.named_scope("weight_b"):
        block = (lax.axis_index("x") * n_zl + lax.axis_index("zl")).astype(jnp.int32)[None]
        got, second_a = call(
            lambda *refs: weight_b_kernel(pairs, *refs), "weight_b", 2 * owned * n_feat * width * width,
            (shape((n_x, n_zl, width + 16, owned), bf16), shape((1, width), f32)),
            block, grads, p_ba, scalars=1,
        )
        got, p_ab = together((got, p_ab))
        got = lax.all_to_all(got, "x", 0, 0, tiled=True)
        p_ab = collect(p_ab, "zl")
        got, p_ab = together((got, p_ab))
        rows_out = got.shape[2]
        got = call(
            lambda *refs: fold_kernel(width, *refs), "fold", 0,
            shape((n_zl, rows_out, owned), bf16), got,
        )
        got = lax.all_to_all(got, "zl", 0, 0, tiled=True)
        turn = lambda r: [(i, (i + r) % n_x) for i in range(n_x)]
        p_ab = [p_ab] + [lax.ppermute(p_ab, "x", turn(r)) for r in range(1, n_x)]

    with jax.named_scope("weight_a"):
        side = call(
            lambda *refs: weight_a_kernel(pairs, *refs), "weight_a", 2 * owned * n_feat * width * width,
            shape((2 * owned + 8, width), f32),
            x_index, *p_ab, grads, plain, inverse, second_a, scalars=1,
        )

    with jax.named_scope("finish"):
        result = call(finish_kernel, "finish", 0, shape((n_feat, sub, width), f32), got, side)
        return result[:, None]


def solution(mesh):
    names = tuple(n for n, _ in SIZES)
    fine = Mesh(mesh.devices.reshape(tuple(s for _, s in SIZES)), names)
    spec = P(DP, FEAT)
    return jax.shard_map(
        body,
        mesh=fine,
        in_specs=(spec, spec, spec, spec),
        out_specs=P(None, DP, None, FEAT),
        check_vma=False,
    )
```
